256 devices in a mesh: queue: 32 (over z, y_hi, core), tp: 8 (over y_lo, x).
Axes of the slice: x: 4, y: 4 (y_hi: 2, y_lo: 2; y = y_hi * 2 + y_lo), z: 8, core: 2. Of those that a mesh axis runs over, the one named last changes fastest.
Arguments:
- latents: bfloat16 [12288, 3072], P('queue'), may hold values from -6 to 6
- fresh_noise: bfloat16 [192, 3072], P(None, 'tp'), may hold values from -6 to 6
- levels: int32 [32], P('queue'), may hold values from 0 to 49, as said below
- frame_counts: int32 [32], P('queue'), may hold values from 1 to 2, as said below
- modulation: float32 [50, 2, 3072], replicated, may hold values from -2.5 to 2.5
- w_qkv: bfloat16 [3072, 3, 3072], P(None, None, 'tp')
- w_out: bfloat16 [3072, 3072], P('tp'), may hold values from -0.109375 to 0.109375
- sampler_coef: float32 [2, 50], replicated, may hold values from -1.2 to 1.2
Outputs:
- queue_next: bfloat16 [12288, 3072], P('queue', 'tp')
- finished: bfloat16 [192, 3072], P('queue', 'tp')
The draws below stay inside these ranges and needn't reach their ends.
Inputs may be any that keep to these rules, and one draw needn't show every extreme that they name: `levels`: levels rise along the queue: group c has a level within one of c * 49 // 31; the first group has 0 and the last 49. `frame_counts`: the first 2 - count frame slots of a group are empty; some group is full and some group has one frame.
All inputs are finite; a program needn't handle non-finite values.
Results may differ from the reference program's by a relative error of at most 0.0075.
The reference program's roundings to bfloat16 on the way (of `normed`, `projected`, `weights` and `attended`) count: a program that leaves them out, or rounds other values in their place, can miss the bound.
Values may be sent and summed in bfloat16 or wider, within the bound.
A program may use at most 64 MiB of HBM per device.

```python
import jax
import jax.numpy as jnp
from jax import lax

D = 3072
HEADS = 48
HEAD_DIM = 64
FRAMES = 2
FRAME_TOK = 192
LEVELS = 50
GROUPS = 32
ROWS = 384
TOKENS = 12288


def draw_levels(key, part):
    key = jax.random.fold_in(key, 11)
    base = jnp.arange(GROUPS, dtype=jnp.int32) * (LEVELS - 1) // (GROUPS - 1)
    jitter = jax.random.randint(key, (GROUPS,), -1, 2, dtype=jnp.int32)
    picked = jnp.clip(base + jitter, 0, LEVELS - 1)
    picked = picked.at[0].set(0)
    picked = picked.at[GROUPS - 1].set(LEVELS - 1)
    return picked.astype(jnp.int32)


def draw_frame_counts(key, part):
    key = jax.random.fold_in(key, 23)
    key_one, key_two, key_three = jax.random.split(key, 3)
    counts = jax.random.randint(key_one, (GROUPS,), 1, FRAMES + 1, dtype=jnp.int32)
    full_at = jax.random.randint(key_two, (), 0, GROUPS, dtype=jnp.int32)
    offset = jax.random.randint(key_three, (), 1, GROUPS, dtype=jnp.int32)
    single_at = (full_at + offset) % GROUPS
    counts = counts.at[full_at].set(FRAMES)
    counts = counts.at[single_at].set(1)
    return counts.astype(jnp.int32)


def draw_w_qkv(key, part):
    key = jax.random.fold_in(key, 37)
    values = jax.random.normal(key, (D, 3, D), jnp.float32) * float(D) ** (-0.5)
    return values.astype(jnp.bfloat16)


def level_of(own_key, extent, cuts, smallest, top_value):
    gain = 1.0
    for dim, blocks in cuts:
        draws = jax.random.uniform(jax.random.fold_in(jax.random.fold_in(own_key, 6), dim), (blocks,), jnp.float32, smallest / len(cuts), top_value / len(cuts))
        gain = gain * jnp.repeat(jnp.exp(draws), extent[dim] // blocks).reshape((-1,) + (1,) * (len(extent) - 1 - dim))
    return gain


def bell_draw(key, dims, scale, reach, cuts=(), kind=jnp.bfloat16):
    entries = jax.random.normal(key, dims, jnp.float32) * scale
    if len(cuts) > 0:
        entries = level_of(key, dims, cuts, -0.22, 0.18) * entries
    return jnp.clip(entries, min=-reach, max=reach).astype(kind)


def setup_inputs(seed: int = 0) -> dict:
    streams_of = jax.random.split(jax.random.key(seed), 9)
    latents = bell_draw(streams_of[0], (TOKENS, D), 1.0, 6.0, ((0, 32),))
    fresh_noise = bell_draw(streams_of[1], (FRAME_TOK, D), 1.0, 6.0, ((1, 8),))
    levels = draw_levels(jax.random.fold_in(streams_of[8], 71), 0)
    frame_counts = draw_frame_counts(jax.random.fold_in(streams_of[8], 71), 0)
    modulation = bell_draw(streams_of[4], (LEVELS, 2, D), 0.5, 2.5, (), jnp.float32)
    w_qkv = draw_w_qkv(jax.random.fold_in(streams_of[8], 71), 0)
    w_out = bell_draw(streams_of[6], (D, D), D ** -0.5, 0.109375, ((0, 8),))
    sampler_coef = jnp.clip(jax.random.uniform(streams_of[7], (2, LEVELS), jnp.float32, -1.2, 1.2), -1.2, 1.2)
    return {"latents": latents, "fresh_noise": fresh_noise, "levels": levels, "frame_counts": frame_counts, "modulation": modulation, "w_qkv": w_qkv, "w_out": w_out, "sampler_coef": sampler_coef}


def normalize(latents, levels, modulation):
    rows_all = latents.astype(jnp.float32).reshape(GROUPS, ROWS, D)
    table = modulation[levels]
    center = lax.optimization_barrier(jnp.mean(rows_all, axis=2, keepdims=True))
    spread = lax.optimization_barrier(jnp.mean((rows_all - center) ** 2, axis=2, keepdims=True))
    normed = (rows_all - center) * lax.rsqrt(spread + 1e-06)
    normed = normed * (1.0 + table[:, 1][:, None, :]) + table[:, 0][:, None, :]
    return normed.astype(jnp.bfloat16).reshape(TOKENS, D)

def reference(latents, fresh_noise, levels, frame_counts, modulation, w_qkv, w_out, sampler_coef):
    normed = normalize(latents, levels, modulation)
    projected = jnp.dot(normed, w_qkv.reshape(D, 3 * D), preferred_element_type=jnp.float32)
    projected = projected.astype(jnp.bfloat16).reshape(GROUPS, ROWS, 3, HEADS, HEAD_DIM)
    last_frames = projected[:, ROWS - FRAME_TOK:]
    prior_all = jnp.concatenate([jnp.zeros_like(last_frames[:1]), last_frames[:-1]], axis=0)
    group_ids = jnp.arange(GROUPS, dtype=jnp.int32)

    def attend_group(packed):
        group_id, own, prior, count = packed
        queries = own[:, 0].astype(jnp.float32)
        key_set = jnp.concatenate([prior[:, 1], own[:, 1]], axis=0).astype(jnp.float32)
        val_set = jnp.concatenate([prior[:, 2], own[:, 2]], axis=0).astype(jnp.float32)
        scores = jnp.einsum('qhd,khd->hqk', queries, key_set) * (1.0 / math_sqrt(HEAD_DIM))
        position = jnp.arange(FRAME_TOK + ROWS, dtype=jnp.int32)
        own_frame = (position - FRAME_TOK) // FRAME_TOK
        live = jnp.where(position < FRAME_TOK, group_id > 0, own_frame >= FRAMES - count)
        masked = jnp.where(live[None, None, :], scores, jnp.float32(-1e+30))
        top = lax.optimization_barrier(jnp.max(masked, axis=2, keepdims=True))
        expo = jnp.exp(masked - top)
        weights = (expo / lax.optimization_barrier(jnp.sum(expo, axis=2, keepdims=True))).astype(jnp.bfloat16)
        attended = jnp.einsum('hqk,khd->qhd', weights.astype(jnp.float32), val_set)
        return attended.astype(jnp.bfloat16).reshape(ROWS, D)
    attended = lax.map(attend_group, (group_ids, projected, prior_all, frame_counts))
    branch = jnp.dot(attended.reshape(TOKENS, D), w_out, preferred_element_type=jnp.float32)
    branch = branch.reshape(GROUPS, ROWS, D)
    current = latents.astype(jnp.float32).reshape(GROUPS, ROWS, D)
    first_coef = sampler_coef[0][levels][:, None, None]
    second_coef = sampler_coef[1][levels][:, None, None]
    updated = first_coef * current + second_coef * (current + branch)
    row_frame = jnp.arange(ROWS, dtype=jnp.int32) // FRAME_TOK
    valid = row_frame[None, :] >= FRAMES - frame_counts[:, None]
    updated = jnp.where(valid[:, :, None], updated, current)
    rounded = updated.astype(jnp.bfloat16)
    leading = rounded[:, :FRAME_TOK]
    arriving = jnp.concatenate([leading[1:], fresh_noise[None]], axis=0)
    queue_next = jnp.concatenate([rounded[:, FRAME_TOK:], arriving], axis=1).reshape(TOKENS, D)
    finished = leading[0]
    return (queue_next, finished)

def math_sqrt(value):
    return float(value) ** 0.5
```

```python
import jax
import jax.numpy as jnp
from jax import lax
from jax.experimental import pallas as pl
from jax.experimental.pallas import tpu as pltpu
from jax.sharding import PartitionSpec as P

MESH = pl.DeviceIdType.MESH
BF = jnp.bfloat16
F32 = jnp.float32
D = 3072
W = 384
ROWS = 384
TOK = 192
NX = 4
C = 128
NC = 3
BIG = 1e30


def kernel(
    nq, levels, counts, coef, lat_hbm, mod_hbm, wqkv_hbm, wout_hbm, fresh_hbm,
    out_ref, fin_ref,
    lat, mod, wbuf, normed, qbuf, kown, vt, kpri, vpri, vtp, wo, fw, ag,
    acc, rsend, rrecv, f0, f0f, arr, finsrc, findst,
    ld_sem, kv_s, kv_r, wo_s, wo_r, ag_s, ag_r, rs_s, rs_r, f_s, f_r, fin_s, fin_r, fresh_sem,
):
    q = lax.axis_index("queue")
    t = lax.axis_index("tp")
    x = lax.rem(t, NX)
    y = t // NX
    xr, xl, xo = lax.rem(x + 1, NX), lax.rem(x + 3, NX), lax.rem(x + 2, NX)
    right, left = y * NX + xr, y * NX + xl
    ypeer = (1 - y) * NX + x
    core = lax.rem(q, 2)
    sib = q + 1 - 2 * core

    def load(src, dst, i):
        return pltpu.make_async_copy(src, dst, ld_sem.at[i])

    def remote(src, dst, ss, rs, **dev):
        return pltpu.make_async_remote_copy(
            src_ref=src, dst_ref=dst, send_sem=ss, recv_sem=rs, device_id=dev, device_id_type=MESH
        )

    ld_f1 = load(lat_hbm.at[pl.ds(TOK, TOK)], lat.at[pl.ds(TOK, TOK)], 0)
    ld_mod = load(mod_hbm, mod, 1)
    ld_k = load(wqkv_hbm.at[1], wbuf.at[:, pl.ds(0, W)], 2)
    ld_v = load(wqkv_hbm.at[2], wbuf.at[:, pl.ds(W, W)], 3)
    ld_f0 = load(lat_hbm.at[pl.ds(0, TOK)], lat.at[pl.ds(0, TOK)], 4)
    ld_q = load(wqkv_hbm.at[0], wbuf.at[:, pl.ds(2 * W, W)], 5)

    def col(block):
        return pl.ds(pl.multiple_of(block * W, 128), W)

    ld_o = [load(wout_hbm.at[:, col(j * NX + x)], wo.at[j, pl.ds(0, W)], 6 + j) for j in range(2)]
    for c in (ld_f1, ld_mod, ld_k, ld_v, ld_f0, ld_q, *ld_o):
        c.start()

    barrier = pltpu.get_barrier_semaphore()
    for dev in ({"tp": right}, {"tp": left}, {"tp": ypeer}):
        pl.semaphore_signal(barrier, inc=1, device_id=dev, device_id_type=MESH)

    @pl.when(q > 0)
    def _():
        pl.semaphore_signal(barrier, inc=1, device_id={"queue": q - 1}, device_id_type=MESH)

    @pl.when(q < nq - 1)
    def _():
        pl.semaphore_signal(barrier, inc=1, device_id={"queue": q + 1}, device_id_type=MESH)

    @pl.when(q > 1)
    def _():
        pl.semaphore_signal(barrier, inc=1, device_id={"queue": 0}, device_id_type=MESH)

    @pl.when(q == 0)
    def _():
        pl.semaphore_wait(barrier, 4 + nq - 2)

    @pl.when((q > 0) & (q < nq - 1))
    def _():
        pl.semaphore_wait(barrier, 5)

    @pl.when(q == nq - 1)
    def _():
        pl.semaphore_wait(barrier, 4)

    wc = wo.at[core]
    H = W // 2
    opp = col(core * NX + xo)
    wo_via_r = remote(wout_hbm.at[pl.ds(0, H), opp], fw.at[0], wo_s.at[2], wo_r.at[2], tp=right)
    wo_via_l = remote(wout_hbm.at[pl.ds(H, H), opp], fw.at[1], wo_s.at[3], wo_r.at[3], tp=left)
    wo_r1 = remote(wout_hbm.at[:, col(core * NX + xr)], wc.at[pl.ds(W, W)], wo_s.at[0], wo_r.at[0], tp=right)
    wo_l1 = remote(wout_hbm.at[:, col(core * NX + xl)], wc.at[pl.ds(3 * W, W)], wo_s.at[1], wo_r.at[1], tp=left)
    wo_fr = remote(fw.at[0], wc.at[pl.ds(2 * W, H)], wo_s.at[4], wo_r.at[4], tp=right)
    wo_fl = remote(fw.at[1], wc.at[pl.ds(2 * W + H, H)], wo_s.at[5], wo_r.at[5], tp=left)
    wo_sib = [
        remote(wc.at[pl.ds(s * W, W)], wc.at[pl.ds(s * W, W)], wo_s.at[5 + s], wo_r.at[5 + s], queue=sib)
        for s in (1, 2, 3)
    ]
    for c in (wo_via_r, wo_via_l, wo_r1, wo_l1):
        c.start()

    level = levels[0]
    count = counts[0]
    full = count == 2
    c_lat = coef[0, level]
    c_out = coef[1, level]

    def norm(start):
        table = mod[level]
        gain = 1.0 + table[1:2]
        shift = table[0:1]

        def step(i, _):
            rows = pl.ds(pl.multiple_of(start + i * 16, 16), 16)
            v = lat[rows, :].astype(F32)
            d = v - jnp.mean(v, axis=1, keepdims=True)
            s = jnp.mean(d * d, axis=1, keepdims=True)
            normed[rows, :] = (d * lax.rsqrt(s + 1e-6) * gain + shift).astype(BF)
            return 0

        lax.fori_loop(0, TOK // 16, step, 0, unroll=2)

    def mm(start, rows, lo, width):
        return jnp.dot(
            normed[pl.ds(start, rows), :], wbuf[:, pl.ds(lo, width)], preferred_element_type=F32
        ).astype(BF)

    kv_k = remote(kown.at[pl.ds(TOK, TOK)], kpri, kv_s.at[0], kv_r.at[0], queue=q + 1)
    kv_v = remote(f0.at[1], vpri, kv_s.at[1], kv_r.at[1], queue=q + 1)

    ld_f1.wait()
    ld_mod.wait()
    norm(TOK)
    ld_k.wait()
    ld_v.wait()
    kown[pl.ds(TOK, TOK), pl.ds(0, 256)] = mm(TOK, TOK, 0, 256)
    mid = mm(TOK, TOK, 256, 256)
    kown[pl.ds(TOK, TOK), pl.ds(256, 128)] = mid[:, :128]

    @pl.when(q < nq - 1)
    def _():
        kv_k.start()

    f0[1, :, pl.ds(0, 128)] = mid[:, 128:]
    f0[1, :, pl.ds(128, 256)] = mm(TOK, TOK, 512, 256)

    @pl.when(q < nq - 1)
    def _():
        kv_v.start()

    @pl.when(q == 0)
    def _():
        kpri[...] = jnp.zeros_like(kpri)
        vpri[...] = jnp.zeros_like(vpri)

    ld_f0.wait()
    norm(0)

    wo_via_r.wait_recv()
    wo_fr.start()
    wo_via_l.wait_recv()
    wo_fl.start()

    ld_q.wait()
    qbuf[:, pl.ds(0, 256)] = mm(0, ROWS, 2 * W, 256) * BF(0.125)
    qbuf[:, pl.ds(256, 128)] = mm(0, ROWS, 2 * W + 256, 128) * BF(0.125)
    kown[pl.ds(0, TOK), pl.ds(0, 256)] = mm(0, TOK, 0, 256)
    mid = mm(0, TOK, 256, 256)
    kown[pl.ds(0, TOK), pl.ds(256, 128)] = mid[:, :128]
    v0 = jnp.concatenate([mid[:, 128:], mm(0, TOK, 512, 256)], axis=1)
    vt[...] = jnp.concatenate([v0, f0[1]], axis=0).T

    lane = lax.broadcasted_iota(jnp.int32, (C, C), 1)
    row = lax.broadcasted_iota(jnp.int32, (C, C), 0)
    has_prior = q > 0
    even = (lane < 64).astype(F32)
    odd = 1.0 - even

    def att_pair(r, p):
        lanes = pl.ds(p * 128, 128)
        qp = qbuf[pl.ds(r * C, C), lanes].astype(F32)
        qs = jnp.concatenate([qp * even, qp * odd], axis=0).astype(BF)
        nt = (((1,), (1,)), ((), ()))
        so = lax.dot_general(kown[:, lanes], qs, nt, preferred_element_type=F32)
        sp = lax.dot_general(kpri[:, lanes], qs, nt, preferred_element_type=F32)
        s0, s1 = so[:TOK], so[TOK:]
        m0 = jnp.where(full, jnp.max(s0, axis=0, keepdims=True), -BIG)
        m1 = jnp.max(s1, axis=0, keepdims=True)
        mp = jnp.where(has_prior, jnp.max(sp, axis=0, keepdims=True), -BIG)
        top = jnp.maximum(jnp.maximum(m0, m1), mp)
        e0 = jnp.exp(s0 - jnp.where(full, top, BIG))
        e1 = jnp.exp(s1 - top)
        ep = jnp.exp(sp - jnp.where(has_prior, top, BIG))
        total = (
            jnp.sum(e0, axis=0, keepdims=True)
            + jnp.sum(e1, axis=0, keepdims=True)
            + jnp.sum(ep, axis=0, keepdims=True)
        )
        inv = 1.0 / total
        w_own = jnp.concatenate([(e0 * inv).astype(BF), (e1 * inv).astype(BF)], axis=0)
        w_pri = (ep * inv).astype(BF)
        o = jnp.dot(vt[lanes, :], w_own, preferred_element_type=F32)
        o = o + jnp.dot(vtp[lanes, :], w_pri, preferred_element_type=F32)
        ot = jnp.where(row < 64, o[:, :C], o[:, C:])
        ag[r, :, lanes] = ot.T.astype(BF)

    ag_dir, ag_fwd = [], []
    for r in range(NC):
        own = ag.at[r, :, pl.ds(0, W)]
        ag_dir.append((
            remote(own, ag.at[r, :, pl.ds(W, W)], ag_s.at[r, 0], ag_r.at[r, 0], tp=right),
            remote(own, ag.at[r, :, pl.ds(3 * W, W)], ag_s.at[r, 1], ag_r.at[r, 1], tp=left),
        ))
        top_half, low_half = pl.ds(0, C // 2), pl.ds(C // 2, C // 2)
        ag_fwd.append((
            remote(ag.at[r, top_half, pl.ds(W, W)], ag.at[r, top_half, pl.ds(2 * W, W)],
                   ag_s.at[r, 2], ag_r.at[r, 2], tp=right),
            remote(ag.at[r, low_half, pl.ds(3 * W, W)], ag.at[r, low_half, pl.ds(2 * W, W)],
                   ag_s.at[r, 3], ag_r.at[r, 3], tp=left),
        ))

    def ag_start(r):
        for c in ag_dir[r]:
            c.start()

    def ag_forward(r):
        for got, on in zip(ag_dir[r], ag_fwd[r]):
            got.wait_recv()
            on.start()

    rs = [remote(rsend.at[r], rrecv.at[r], rs_s.at[r], rs_r.at[r], tp=ypeer) for r in range(NC)]

    def proj(r):
        for c in ag_fwd[r]:
            c.wait_recv()
        a = ag[r]
        rsend[r] = jnp.dot(a, wo[1 - y], preferred_element_type=F32).astype(BF)
        rs[r].start()
        acc[r] = jnp.dot(a, wo[y], preferred_element_type=F32)

    def final(r):
        rs[r].wait_recv()
        branch = acc[r] + rrecv[r].astype(F32)
        cur = lat[pl.ds(r * C, C), col(t)].astype(F32)
        upd = c_lat * cur + c_out * (cur + branch)
        if r == 0:
            valid = full
        elif r == 2:
            valid = True
        else:
            valid = full | (lax.broadcasted_iota(jnp.int32, (C, W), 0) >= TOK - C)
        if valid is not True:
            upd = jnp.where(valid, upd, cur)
        return upd

    @pl.when(q > 0)
    def _():
        kv_k.wait_recv()
        kv_v.wait_recv()

    vtp[...] = vpri[...].T

    for p in range(3):
        att_pair(0, p)
    ag_start(0)
    wo_r1.wait_recv()
    wo_sib[0].start()
    for p in range(3):
        att_pair(1, p)
        if p == 0:
            ag_forward(0)
    ag_start(1)
    wo_l1.wait_recv()
    wo_sib[2].start()
    wo_fr.wait_recv()
    wo_fl.wait_recv()
    wo_sib[1].start()
    att_pair(2, 0)
    ag_forward(1)
    for c in ld_o:
        c.wait()
    for c in wo_sib:
        c.wait_recv()
    proj(0)
    att_pair(2, 1)
    att_pair(2, 2)
    ag_start(2)
    proj(1)
    ag_forward(2)

    f_a = remote(f0.at[0, pl.ds(0, C)], arr.at[pl.ds(0, C)], f_s.at[0], f_r.at[0], queue=q - 1)
    f_b = remote(
        f0.at[0, pl.ds(C, TOK - C)], arr.at[pl.ds(C, TOK - C)], f_s.at[1], f_r.at[1], queue=q - 1
    )
    fresh = pltpu.make_async_copy(fresh_hbm, arr, fresh_sem)

    @pl.when(q == nq - 1)
    def _():
        fresh.start()

    u = final(0)
    f0[0, pl.ds(0, C)] = u.astype(BF)
    f0f[pl.ds(0, C)] = u

    @pl.when(q > 0)
    def _():
        f_a.start()

    proj(2)
    u = final(1)
    f0[0, pl.ds(C, TOK - C)] = u[: TOK - C].astype(BF)
    f0f[pl.ds(C, TOK - C)] = u[: TOK - C]
    out_ref[pl.ds(0, 2 * C - TOK)] = u[TOK - C :].astype(BF)

    @pl.when(q > 0)
    def _():
        f_b.start()

    share = TOK // nq

    def fin_copy(i):
        return remote(finsrc.at[i], findst, fin_s.at[i], fin_r.at[0], queue=i)

    @pl.when(q == 0)
    def _():
        f0f[pl.ds(TOK, 16)] = jnp.zeros((16, W), F32)
        for i in range(nq):
            finsrc[i] = f0f[pl.ds(i * share, 16)].astype(BF)

        def go(i, _):
            fin_copy(i).start()
            return 0

        lax.fori_loop(1, nq, go, 0)

    out_ref[pl.ds(2 * C - TOK, C)] = final(2).astype(BF)

    @pl.when(q > 0)
    def _():
        f_a.wait_send()
        f_b.wait_send()
        fin_copy(0).wait_recv()
        fin_ref[...] = findst[pl.ds(0, share)]

    @pl.when(q == 0)
    def _():
        fin_ref[...] = finsrc[0, pl.ds(0, share)]

        def done(i, _):
            fin_copy(i).wait_send()
            return 0

        lax.fori_loop(1, nq, done, 0)

    @pl.when(q < nq - 1)
    def _():
        kv_k.wait_send()
        kv_v.wait_send()
        f_a.wait_recv()
        f_b.wait_recv()

    @pl.when(q == nq - 1)
    def _():
        fresh.wait()

    out_ref[pl.ds(TOK, TOK)] = arr[...]
    for c in (wo_via_r, wo_via_l, wo_r1, wo_l1, wo_fr, wo_fl, *wo_sib, *rs):
        c.wait_send()
    for r in range(NC):
        for c in (*ag_dir[r], *ag_fwd[r]):
            c.wait_send()


def solution(mesh):
    nq = mesh.shape["queue"]

    def step(latents, fresh_noise, levels, frame_counts, modulation, w_qkv, w_out, sampler_coef):
        anyspace = pl.BlockSpec(memory_space=pl.ANY)
        smem = pl.BlockSpec(memory_space=pltpu.SMEM)
        vmem = pl.BlockSpec(memory_space=pltpu.VMEM)
        dma = pltpu.SemaphoreType.DMA
        return pl.pallas_call(
            lambda *refs: kernel(nq, *refs),
            out_shape=(
                jax.ShapeDtypeStruct((ROWS, W), BF),
                jax.ShapeDtypeStruct((TOK // nq, W), BF),
            ),
            in_specs=[smem, smem, smem] + [anyspace] * 5,
            out_specs=(vmem, vmem),
            scratch_shapes=[
                pltpu.VMEM((ROWS, D), BF),
                pltpu.VMEM(modulation.shape, F32),
                pltpu.VMEM((D, 3 * W), BF),
                pltpu.VMEM((ROWS, D), BF),
                pltpu.VMEM((ROWS, W), BF),
                pltpu.VMEM((ROWS, W), BF),
                pltpu.VMEM((W, ROWS), BF),
                pltpu.VMEM((TOK, W), BF),
                pltpu.VMEM((TOK, W), BF),
                pltpu.VMEM((W, TOK), BF),
                pltpu.VMEM((2, NX * W, W), BF),
                pltpu.VMEM((2, W // 2, W), BF),
                pltpu.VMEM((NC, C, NX * W), BF),
                pltpu.VMEM((NC, C, W), F32),
                pltpu.VMEM((NC, C, W), BF),
                pltpu.VMEM((NC, C, W), BF),
                pltpu.VMEM((2, TOK, W), BF),
                pltpu.VMEM((TOK + 16, W), F32),
                pltpu.VMEM((TOK, W), BF),
                pltpu.VMEM((nq, 16, W), BF),
                pltpu.VMEM((16, W), BF),
                dma((8,)), dma((2,)), dma((2,)), dma((9,)), dma((9,)),
                dma((NC, 4)), dma((NC, 4)), dma((NC,)), dma((NC,)),
                dma((2,)), dma((2,)), dma((nq,)), dma((1,)), dma,
            ],
            compiler_params=pltpu.CompilerParams(
                collective_id=0, has_side_effects=True, vmem_limit_bytes=56 * 1024 * 1024
            ),
        )(
            levels, frame_counts, sampler_coef, latents, modulation,
            jnp.transpose(w_qkv, (1, 0, 2)), w_out, fresh_noise,
        )

    return jax.shard_map(
        step,
        mesh=mesh,
        in_specs=(
            P("queue", None), P(None, "tp"), P("queue"), P("queue"), P(),
            P(None, None, "tp"), P("tp", None), P(),
        ),
        out_specs=(P("queue", "tp"), P("queue", "tp")),
        check_vma=False,
    )
```

```python
import jax
import jax.numpy as jnp
from jax import lax
from jax.experimental import pallas as pl
from jax.experimental.pallas import tpu as pltpu
from jax.sharding import PartitionSpec as P

MESH = pl.DeviceIdType.MESH
BF = jnp.bfloat16
F32 = jnp.float32
D = 3072
W = 384
ROWS = 384
TOK = 192
NX = 4
C = 128
NC = 3
BIG = 1e30


def kernel(
    nq, levels, counts, coef, lat_hbm, mod_hbm, wqkv_hbm, wout_hbm, fresh_hbm,
    out_ref, fin_ref,
    lat, mod, wbuf, normed, qbuf, kown, vt, kpri, vpri, vtp, wo, ag,
    acc, rsend, rrecv, f0, f0f, arr, finsrc, findst,
    ld_sem, kv_s, kv_r, wo_s, wo_r, ag_s, ag_r, rs_s, rs_r, f_s, f_r, fin_s, fin_r, fresh_sem, here,
):
    q = lax.axis_index("queue")
    t = lax.axis_index("tp")
    x = lax.rem(t, NX)
    y = t // NX
    xr, xl, xo = lax.rem(x + 1, NX), lax.rem(x + 3, NX), lax.rem(x + 2, NX)
    right, left, opposite = y * NX + xr, y * NX + xl, y * NX + xo
    ypeer = (1 - y) * NX + x
    core = lax.rem(q, 2)
    sib = q + 1 - 2 * core

    def load(src, dst, i):
        return pltpu.make_async_copy(src, dst, ld_sem.at[i])

    def remote(src, dst, ss, rs, **dev):
        return pltpu.make_async_remote_copy(
            src_ref=src, dst_ref=dst, send_sem=ss, recv_sem=rs, device_id=dev, device_id_type=MESH
        )

    ld_f1 = load(lat_hbm.at[pl.ds(TOK, TOK)], lat.at[pl.ds(TOK, TOK)], 0)
    ld_mod = load(mod_hbm, mod, 1)
    ld_k = load(wqkv_hbm.at[1], wbuf.at[:, pl.ds(0, W)], 2)
    ld_v = load(wqkv_hbm.at[2], wbuf.at[:, pl.ds(W, W)], 3)
    ld_f0 = load(lat_hbm.at[pl.ds(0, TOK)], lat.at[pl.ds(0, TOK)], 4)
    ld_q = load(wqkv_hbm.at[0], wbuf.at[:, pl.ds(2 * W, W)], 5)

    def col(block):
        return pl.ds(pl.multiple_of(block * W, 128), W)

    def wblock(half, k):
        return wout_hbm.at[:, col(half * NX + k)]

    ld_o = [load(wblock(y, k), wo.at[k, pl.ds(0, W)], 6 + k) for k in range(NX)]
    for c in (ld_f1, ld_mod, ld_k, ld_v, ld_f0, ld_q, *ld_o):
        c.start()

    barrier = pltpu.get_barrier_semaphore()

    def hello(**dev):
        pl.semaphore_signal(barrier, inc=1, device_id=dev, device_id_type=MESH)

    for peer in (right, left, opposite, ypeer):
        hello(tp=peer)

    @pl.when(q == 0)
    def _():
        def greet(i, _):
            hello(queue=i)
            return 0

        lax.fori_loop(1, nq, greet, 0)

    @pl.when(q > 0)
    def _():
        hello(queue=q - 1)

        @pl.when(q < nq - 1)
        def _():
            hello(queue=q + 1)

    def meet():
        @pl.when(q == 0)
        def _():
            pl.semaphore_wait(barrier, 5)

        @pl.when(q == 1)
        def _():
            pl.semaphore_wait(barrier, 6)

        @pl.when((q > 1) & (q < nq - 1))
        def _():
            pl.semaphore_wait(barrier, 7)

        @pl.when(q == nq - 1)
        def _():
            pl.semaphore_wait(barrier, 6)

        @pl.when(q > 0)
        def _():
            pl.semaphore_signal(here, inc=1, device_id={"queue": 0}, device_id_type=MESH)

    wo_y, wo_sib = [], []
    for i in range(2):
        k = 2 * core + i
        low = wo.at[k, pl.ds(W, W)]
        wo_y.append(remote(wblock(1 - y, k), low, wo_s.at[i], wo_r.at[i], tp=ypeer))
        wo_sib.append(remote(low, low, wo_s.at[2 + i], wo_r.at[2 + i], queue=sib))

    level = levels[0]
    count = counts[0]
    full = count == 2
    c_lat = coef[0, level]
    c_out = coef[1, level]

    def norm(start):
        table = mod[level]
        gain = 1.0 + table[1:2]
        shift = table[0:1]

        def step(i, _):
            rows = pl.ds(pl.multiple_of(start + i * 16, 16), 16)
            v = lat[rows, :].astype(F32)
            d = v - jnp.mean(v, axis=1, keepdims=True)
            s = jnp.mean(d * d, axis=1, keepdims=True)
            normed[rows, :] = (d * lax.rsqrt(s + 1e-6) * gain + shift).astype(BF)
            return 0

        lax.fori_loop(0, TOK // 16, step, 0, unroll=2)

    def mm(start, rows, lo, width):
        return jnp.dot(
            normed[pl.ds(start, rows), :], wbuf[:, pl.ds(lo, width)], preferred_element_type=F32
        ).astype(BF)

    kv_k = remote(kown.at[pl.ds(TOK, TOK)], kpri, kv_s.at[0], kv_r.at[0], queue=q + 1)
    kv_v = remote(f0.at[1], vpri, kv_s.at[1], kv_r.at[1], queue=q + 1)

    ld_f1.wait()
    ld_mod.wait()
    norm(TOK)
    ld_k.wait()
    ld_v.wait()
    kown[pl.ds(TOK, TOK), pl.ds(0, 256)] = mm(TOK, TOK, 0, 256)
    mid = mm(TOK, TOK, 256, 256)
    kown[pl.ds(TOK, TOK), pl.ds(256, 128)] = mid[:, :128]
    meet()

    @pl.when(q < nq - 1)
    def _():
        kv_k.start()

    for c in wo_y:
        c.start()
    f0[1, :, pl.ds(0, 128)] = mid[:, 128:]
    f0[1, :, pl.ds(128, 256)] = mm(TOK, TOK, 512, 256)

    @pl.when(q < nq - 1)
    def _():
        kv_v.start()

    @pl.when(q == 0)
    def _():
        kpri[...] = jnp.zeros_like(kpri)
        vpri[...] = jnp.zeros_like(vpri)

    ld_f0.wait()
    norm(0)

    ld_q.wait()
    qbuf[:, pl.ds(0, 256)] = mm(0, ROWS, 2 * W, 256) * BF(0.125)
    qbuf[:, pl.ds(256, 128)] = mm(0, ROWS, 2 * W + 256, 128) * BF(0.125)
    kown[pl.ds(0, TOK), pl.ds(0, 256)] = mm(0, TOK, 0, 256)
    mid = mm(0, TOK, 256, 256)
    kown[pl.ds(0, TOK), pl.ds(256, 128)] = mid[:, :128]
    v0 = jnp.concatenate([mid[:, 128:], mm(0, TOK, 512, 256)], axis=1)
    vt[...] = jnp.concatenate([v0, f0[1]], axis=0).T

    lane = lax.broadcasted_iota(jnp.int32, (C, C), 1)
    row = lax.broadcasted_iota(jnp.int32, (C, C), 0)
    has_prior = q > 0
    even = (lane < 64).astype(F32)
    odd = 1.0 - even

    def att_pair(r, p):
        lanes = pl.ds(p * 128, 128)
        qp = qbuf[pl.ds(r * C, C), lanes].astype(F32)
        qs = jnp.concatenate([qp * even, qp * odd], axis=0).astype(BF)
        nt = (((1,), (1,)), ((), ()))
        so = lax.dot_general(kown[:, lanes], qs, nt, preferred_element_type=F32)
        sp = lax.dot_general(kpri[:, lanes], qs, nt, preferred_element_type=F32)
        s0, s1 = so[:TOK], so[TOK:]
        m0 = jnp.where(full, jnp.max(s0, axis=0, keepdims=True), -BIG)
        m1 = jnp.max(s1, axis=0, keepdims=True)
        mp = jnp.where(has_prior, jnp.max(sp, axis=0, keepdims=True), -BIG)
        top = jnp.maximum(jnp.maximum(m0, m1), mp)
        e0 = jnp.exp(s0 - jnp.where(full, top, BIG))
        e1 = jnp.exp(s1 - top)
        ep = jnp.exp(sp - jnp.where(has_prior, top, BIG))
        total = (
            jnp.sum(e0, axis=0, keepdims=True)
            + jnp.sum(e1, axis=0, keepdims=True)
            + jnp.sum(ep, axis=0, keepdims=True)
        )
        inv = 1.0 / total
        w_own = jnp.concatenate([(e0 * inv).astype(BF), (e1 * inv).astype(BF)], axis=0)
        w_pri = (ep * inv).astype(BF)
        o = jnp.dot(vt[lanes, :], w_own, preferred_element_type=F32)
        o = o + jnp.dot(vtp[lanes, :], w_pri, preferred_element_type=F32)
        ot = jnp.where(row < 64, o[:, :C], o[:, C:])
        ag[r, :, lanes] = ot.T.astype(BF)

    ag_y = [
        remote(ag.at[r, :, pl.ds(0, W)], ag.at[r, :, pl.ds(W, W)], ag_s.at[r], ag_r.at[r], tp=ypeer)
        for r in range(NC)
    ]
    rs = [
        [
            (k, remote(rsend.at[r, i], rrecv.at[r, i], rs_s.at[r, i], rs_r.at[r, i], tp=dev))
            for i, (k, dev) in enumerate(((xo, opposite), (xr, right), (xl, left)))
        ]
        for r in range(NC)
    ]

    def proj(r):
        ag_y[r].wait_recv()
        a = ag[r]
        for i, (k, c) in enumerate(rs[r]):
            rsend[r, i] = jnp.dot(a, wo[k], preferred_element_type=F32).astype(BF)
            c.start()
        acc[r] = jnp.dot(a, wo[x], preferred_element_type=F32)

    def final(r):
        branch = acc[r]
        for i, (_, c) in enumerate(rs[r]):
            c.wait_recv()
            branch = branch + rrecv[r, i].astype(F32)
        cur = lat[pl.ds(r * C, C), col(t)].astype(F32)
        upd = c_lat * cur + c_out * (cur + branch)
        if r == 0:
            valid = full
        elif r == 2:
            valid = True
        else:
            valid = full | (lax.broadcasted_iota(jnp.int32, (C, W), 0) >= TOK - C)
        if valid is not True:
            upd = jnp.where(valid, upd, cur)
        return upd

    @pl.when(q > 0)
    def _():
        kv_k.wait_recv()
        kv_v.wait_recv()

    vtp[...] = vpri[...].T

    for p in range(3):
        att_pair(0, p)
    ag_y[0].start()
    for got, on in zip(wo_y, wo_sib):
        got.wait_recv()
        on.start()
    for p in range(3):
        att_pair(1, p)
    ag_y[1].start()
    for c in ld_o:
        c.wait()
    for c in wo_sib:
        c.wait_recv()
    proj(0)
    for p in range(3):
        att_pair(2, p)
    ag_y[2].start()
    proj(1)
    proj(2)

    f_a = remote(f0.at[0, pl.ds(0, C)], arr.at[pl.ds(0, C)], f_s.at[0], f_r.at[0], queue=q - 1)
    f_b = remote(
        f0.at[0, pl.ds(C, TOK - C)], arr.at[pl.ds(C, TOK - C)], f_s.at[1], f_r.at[1], queue=q - 1
    )
    fresh = pltpu.make_async_copy(fresh_hbm, arr, fresh_sem)

    @pl.when(q == nq - 1)
    def _():
        fresh.start()

    u = final(0)
    f0[0, pl.ds(0, C)] = u.astype(BF)
    f0f[pl.ds(0, C)] = u

    @pl.when(q > 0)
    def _():
        f_a.start()

    u = final(1)
    f0[0, pl.ds(C, TOK - C)] = u[: TOK - C].astype(BF)
    f0f[pl.ds(C, TOK - C)] = u[: TOK - C]
    out_ref[pl.ds(0, 2 * C - TOK)] = u[TOK - C :].astype(BF)

    @pl.when(q > 0)
    def _():
        f_b.start()

    share = TOK // nq

    def fin_copy(i):
        return remote(finsrc.at[i], findst, fin_s.at[i], fin_r.at[0], queue=i)

    @pl.when(q == 0)
    def _():
        f0f[pl.ds(TOK, 16)] = jnp.zeros((16, W), F32)
        for i in range(nq):
            finsrc[i] = f0f[pl.ds(i * share, 16)].astype(BF)

        def go(i, _):
            fin_copy(i).start()
            return 0

        pl.semaphore_wait(here, nq - 1)
        lax.fori_loop(1, nq, go, 0)

    out_ref[pl.ds(2 * C - TOK, C)] = final(2).astype(BF)

    @pl.when(q > 0)
    def _():
        f_a.wait_send()
        f_b.wait_send()
        fin_copy(0).wait_recv()
        fin_ref[...] = findst[pl.ds(0, share)]

    @pl.when(q == 0)
    def _():
        fin_ref[...] = finsrc[0, pl.ds(0, share)]

        def done(i, _):
            fin_copy(i).wait_send()
            return 0

        lax.fori_loop(1, nq, done, 0)

    @pl.when(q < nq - 1)
    def _():
        kv_k.wait_send()
        kv_v.wait_send()
        f_a.wait_recv()
        f_b.wait_recv()

    @pl.when(q == nq - 1)
    def _():
        fresh.wait()

    out_ref[pl.ds(TOK, TOK)] = arr[...]
    for c in (*wo_y, *wo_sib, *ag_y):
        c.wait_send()
    for r in range(NC):
        for _, c in rs[r]:
            c.wait_send()


def solution(mesh):
    nq = mesh.shape["queue"]

    def step(latents, fresh_noise, levels, frame_counts, modulation, w_qkv, w_out, sampler_coef):
        anyspace = pl.BlockSpec(memory_space=pl.ANY)
        smem = pl.BlockSpec(memory_space=pltpu.SMEM)
        vmem = pl.BlockSpec(memory_space=pltpu.VMEM)
        dma = pltpu.SemaphoreType.DMA
        return pl.pallas_call(
            lambda *refs: kernel(nq, *refs),
            out_shape=(
                jax.ShapeDtypeStruct((ROWS, W), BF),
                jax.ShapeDtypeStruct((TOK // nq, W), BF),
            ),
            in_specs=[smem, smem, smem] + [anyspace] * 5,
            out_specs=(vmem, vmem),
            scratch_shapes=[
                pltpu.VMEM((ROWS, D), BF),
                pltpu.VMEM(modulation.shape, F32),
                pltpu.VMEM((D, 3 * W), BF),
                pltpu.VMEM((ROWS, D), BF),
                pltpu.VMEM((ROWS, W), BF),
                pltpu.VMEM((ROWS, W), BF),
                pltpu.VMEM((W, ROWS), BF),
                pltpu.VMEM((TOK, W), BF),
                pltpu.VMEM((TOK, W), BF),
                pltpu.VMEM((W, TOK), BF),
                pltpu.VMEM((NX, 2 * W, W), BF),
                pltpu.VMEM((NC, C, 2 * W), BF),
                pltpu.VMEM((NC, C, W), F32),
                pltpu.VMEM((NC, 3, C, W), BF),
                pltpu.VMEM((NC, 3, C, W), BF),
                pltpu.VMEM((2, TOK, W), BF),
                pltpu.VMEM((TOK + 16, W), F32),
                pltpu.VMEM((TOK, W), BF),
                pltpu.VMEM((nq, 16, W), BF),
                pltpu.VMEM((16, W), BF),
                dma((10,)), dma((2,)), dma((2,)), dma((4,)), dma((4,)),
                dma((NC,)), dma((NC,)), dma((NC, 3)), dma((NC, 3)),
                dma((2,)), dma((2,)), dma((nq,)), dma((1,)), dma, pltpu.SemaphoreType.REGULAR,
            ],
            compiler_params=pltpu.CompilerParams(
                collective_id=0, has_side_effects=True, vmem_limit_bytes=56 * 1024 * 1024
            ),
        )(
            levels, frame_counts, sampler_coef, latents, modulation,
            jnp.transpose(w_qkv, (1, 0, 2)), w_out, fresh_noise,
        )

    return jax.shard_map(
        step,
        mesh=mesh,
        in_specs=(
            P("queue", None), P(None, "tp"), P("queue"), P("queue"), P(),
            P(None, None, "tp"), P("tp", None), P(),
        ),
        out_specs=(P("queue", "tp"), P("queue", "tp")),
        check_vma=False,
    )
```

```python
import jax
import jax.numpy as jnp
from jax import lax
from jax.experimental import pallas as pl
from jax.experimental.pallas import tpu as pltpu
from jax.sharding import PartitionSpec as P

MESH = pl.DeviceIdType.MESH
BF = jnp.bfloat16
F32 = jnp.float32
D = 3072
W = 384
ROWS = 384
TOK = 192
NX = 4
C = 128
NC = 3
BIG = 1e30


def kernel(
    nq, levels, counts, coef, lat_hbm, mod_hbm, wqkv_hbm, wout_hbm, fresh_hbm,
    out_ref, fin_ref,
    lat, mod, wbuf, normed, qbuf, kown, vt, kpri, vpri, vtp, wo, wst, ag,
    acc, rsend, rrecv, f0, f0f, arr, finsrc, findst,
    ld_sem, kv_s, kv_r, wo_s, wo_r, ag_s, ag_r, rs_s, rs_r, f_s, f_r, fin_s, fin_r, fresh_sem, here,
):
    q = lax.axis_index("queue")
    t = lax.axis_index("tp")
    x = lax.rem(t, NX)
    y = t // NX
    xr, xl, xo = lax.rem(x + 1, NX), lax.rem(x + 3, NX), lax.rem(x + 2, NX)
    right, left, opposite = y * NX + xr, y * NX + xl, y * NX + xo
    ypeer = (1 - y) * NX + x
    core = lax.rem(q, 2)
    sib = q + 1 - 2 * core
    q_other = q + 2 - 4 * (lax.rem(q, 4) // 2)

    def load(src, dst, i):
        return pltpu.make_async_copy(src, dst, ld_sem.at[i])

    def remote(src, dst, ss, rs, **dev):
        return pltpu.make_async_remote_copy(
            src_ref=src, dst_ref=dst, send_sem=ss, recv_sem=rs, device_id=dev, device_id_type=MESH
        )

    ld_f1 = load(lat_hbm.at[pl.ds(TOK, TOK)], lat.at[pl.ds(TOK, TOK)], 0)
    n_levels = mod_hbm.shape[0]
    first = jnp.clip(q * (n_levels - 1) // (nq - 1) - 1, 0, n_levels - 3)
    ld_mod = load(mod_hbm.at[pl.ds(first, 3)], mod, 1)
    ld_k = load(wqkv_hbm.at[1], wbuf.at[:, pl.ds(0, W)], 2)
    ld_v = load(wqkv_hbm.at[2], wbuf.at[:, pl.ds(W, W)], 3)
    ld_f0 = load(lat_hbm.at[pl.ds(0, TOK)], lat.at[pl.ds(0, TOK)], 4)
    ld_q = load(wqkv_hbm.at[0], wbuf.at[:, pl.ds(2 * W, W)], 5)

    def col(block):
        return pl.ds(pl.multiple_of(block * W, 128), W)

    def wblock(half, k):
        return wout_hbm.at[:, col(half * NX + k)]

    ld_o = [load(wblock(y, k), wo.at[k, pl.ds(0, W)], 6 + k) for k in range(NX)]
    ld_w = [load(wblock(1 - y, 2 * core + i), wst.at[i], 10 + i) for i in range(2)]
    for c in (ld_f1, ld_mod, *ld_w, ld_k, ld_v, ld_f0, ld_q, *ld_o):
        c.start()

    barrier = pltpu.get_barrier_semaphore()

    def hello(**dev):
        pl.semaphore_signal(barrier, inc=1, device_id=dev, device_id_type=MESH)

    for peer in (right, left, opposite, ypeer):
        hello(tp=peer)
    hello(tp=ypeer, queue=q_other)

    @pl.when(q == 0)
    def _():
        def greet(i, _):
            hello(queue=i)
            return 0

        lax.fori_loop(1, nq, greet, 0)

    @pl.when(q > 0)
    def _():
        hello(queue=q - 1)

        @pl.when(q < nq - 1)
        def _():
            hello(queue=q + 1)

    def meet():
        @pl.when(q == 0)
        def _():
            pl.semaphore_wait(barrier, 6)

        @pl.when(q == 1)
        def _():
            pl.semaphore_wait(barrier, 7)

        @pl.when((q > 1) & (q < nq - 1))
        def _():
            pl.semaphore_wait(barrier, 8)

        @pl.when(q == nq - 1)
        def _():
            pl.semaphore_wait(barrier, 7)

        @pl.when(q > 0)
        def _():
            pl.semaphore_signal(here, inc=1, device_id={"queue": 0}, device_id_type=MESH)

    wo_y, wo_sib = [], []
    for i in range(2):
        k = 2 * core + i
        low = wo.at[k, pl.ds(W, W)]
        wo_y.append(remote(wst.at[i], low, wo_s.at[i], wo_r.at[i], tp=ypeer, queue=(q, q_other)[i]))
        wo_sib.append(remote(low, low, wo_s.at[2 + i], wo_r.at[2 + i], queue=sib))

    level = levels[0]
    count = counts[0]
    full = count == 2
    c_lat = coef[0, level]
    c_out = coef[1, level]

    def norm(start):
        table = mod[jnp.clip(level - first, 0, 2)]
        gain = 1.0 + table[1:2]
        shift = table[0:1]

        def step(i, _):
            rows = pl.ds(pl.multiple_of(start + i * 16, 16), 16)
            v = lat[rows, :].astype(F32)
            d = v - jnp.mean(v, axis=1, keepdims=True)
            s = jnp.mean(d * d, axis=1, keepdims=True)
            normed[rows, :] = (d * lax.rsqrt(s + 1e-6) * gain + shift).astype(BF)
            return 0

        lax.fori_loop(0, TOK // 16, step, 0, unroll=2)

    def mm(start, rows, lo, width):
        return jnp.dot(
            normed[pl.ds(start, rows), :], wbuf[:, pl.ds(lo, width)], preferred_element_type=F32
        ).astype(BF)

    kv_k = remote(kown.at[pl.ds(TOK, TOK)], kpri, kv_s.at[0], kv_r.at[0], queue=q + 1)
    kv_v = remote(f0.at[1], vpri, kv_s.at[1], kv_r.at[1], queue=q + 1)

    ld_f1.wait()
    ld_mod.wait()
    meet()
    for c, l in zip(wo_y, ld_w):
        l.wait()
        c.start()
    norm(TOK)
    ld_k.wait()
    ld_v.wait()
    kown[pl.ds(TOK, TOK), pl.ds(0, 256)] = mm(TOK, TOK, 0, 256)
    mid = mm(TOK, TOK, 256, 256)
    kown[pl.ds(TOK, TOK), pl.ds(256, 128)] = mid[:, :128]

    @pl.when(q < nq - 1)
    def _():
        kv_k.start()

    f0[1, :, pl.ds(0, 128)] = mid[:, 128:]
    f0[1, :, pl.ds(128, 256)] = mm(TOK, TOK, 512, 256)

    @pl.when(q < nq - 1)
    def _():
        kv_v.start()

    @pl.when(q == 0)
    def _():
        kpri[...] = jnp.zeros_like(kpri)
        vpri[...] = jnp.zeros_like(vpri)

    ld_f0.wait()
    norm(0)

    ld_q.wait()
    qbuf[:, pl.ds(0, 256)] = mm(0, ROWS, 2 * W, 256) * BF(0.125)
    qbuf[:, pl.ds(256, 128)] = mm(0, ROWS, 2 * W + 256, 128) * BF(0.125)
    kown[pl.ds(0, TOK), pl.ds(0, 256)] = mm(0, TOK, 0, 256)
    mid = mm(0, TOK, 256, 256)
    kown[pl.ds(0, TOK), pl.ds(256, 128)] = mid[:, :128]
    v0 = jnp.concatenate([mid[:, 128:], mm(0, TOK, 512, 256)], axis=1)
    vt[...] = jnp.concatenate([v0, f0[1]], axis=0).T

    lane = lax.broadcasted_iota(jnp.int32, (C, C), 1)
    row = lax.broadcasted_iota(jnp.int32, (C, C), 0)
    has_prior = q > 0
    even = (lane < 64).astype(F32)
    odd = 1.0 - even

    def weigh(r, p):
        lanes = pl.ds(p * 128, 128)
        qp = qbuf[pl.ds(r * C, C), lanes].astype(F32)
        qs = jnp.concatenate([qp * even, qp * odd], axis=0).astype(BF)
        nt = (((1,), (1,)), ((), ()))
        so = lax.dot_general(kown[:, lanes], qs, nt, preferred_element_type=F32)
        sp = lax.dot_general(kpri[:, lanes], qs, nt, preferred_element_type=F32)
        s0, s1 = so[:TOK], so[TOK:]
        m0 = jnp.where(full, jnp.max(s0, axis=0, keepdims=True), -BIG)
        m1 = jnp.max(s1, axis=0, keepdims=True)
        mp = jnp.where(has_prior, jnp.max(sp, axis=0, keepdims=True), -BIG)
        top = jnp.maximum(jnp.maximum(m0, m1), mp)
        e0 = jnp.exp(s0 - jnp.where(full, top, BIG))
        e1 = jnp.exp(s1 - top)
        ep = jnp.exp(sp - jnp.where(has_prior, top, BIG))
        total = (
            jnp.sum(e0, axis=0, keepdims=True)
            + jnp.sum(e1, axis=0, keepdims=True)
            + jnp.sum(ep, axis=0, keepdims=True)
        )
        inv = 1.0 / total
        w_own = jnp.concatenate([(e0 * inv).astype(BF), (e1 * inv).astype(BF)], axis=0)
        return w_own, (ep * inv).astype(BF)

    def attend(r, p, w_own, w_pri):
        lanes = pl.ds(p * 128, 128)
        o = jnp.dot(vt[lanes, :], w_own, preferred_element_type=F32)
        o = o + jnp.dot(vtp[lanes, :], w_pri, preferred_element_type=F32)
        ot = jnp.where(row < 64, o[:, :C], o[:, C:])
        ag[r, :, lanes] = ot.T.astype(BF)

    def att_pair(r, p):
        attend(r, p, *weigh(r, p))

    ag_y = [
        remote(ag.at[r, :, pl.ds(0, W)], ag.at[r, :, pl.ds(W, W)], ag_s.at[r], ag_r.at[r], tp=ypeer)
        for r in range(NC)
    ]
    rs = [
        [
            (k, remote(rsend.at[r, i], rrecv.at[r, i], rs_s.at[r, i], rs_r.at[r, i], tp=dev))
            for i, (k, dev) in enumerate(((xo, opposite), (xr, right), (xl, left)))
        ]
        for r in range(NC)
    ]

    def proj(r):
        ag_y[r].wait_recv()
        a = ag[r]
        for i, (k, c) in enumerate(rs[r]):
            rsend[r, i] = jnp.dot(a, wo[k], preferred_element_type=F32).astype(BF)
            c.start()
        acc[r] = jnp.dot(a, wo[x], preferred_element_type=F32)

    def final(r):
        branch = acc[r]
        for i, (_, c) in enumerate(rs[r]):
            c.wait_recv()
            branch = branch + rrecv[r, i].astype(F32)
        cur = lat[pl.ds(r * C, C), col(t)].astype(F32)
        upd = c_lat * cur + c_out * (cur + branch)
        if r == 0:
            valid = full
        elif r == 2:
            valid = True
        else:
            valid = full | (lax.broadcasted_iota(jnp.int32, (C, W), 0) >= TOK - C)
        if valid is not True:
            upd = jnp.where(valid, upd, cur)
        return upd

    @pl.when(q > 0)
    def _():
        kv_k.wait_recv()

    got = weigh(0, 0)

    @pl.when(q > 0)
    def _():
        kv_v.wait_recv()

    vtp[...] = vpri[...].T
    attend(0, 0, *got)
    att_pair(0, 1)
    att_pair(0, 2)
    ag_y[0].start()
    for got, on in zip(wo_y, wo_sib):
        got.wait_recv()
        on.start()
    for p in range(3):
        att_pair(1, p)
    ag_y[1].start()
    for c in ld_o:
        c.wait()
    att_pair(2, 0)
    for c in wo_sib:
        c.wait_recv()
    proj(0)
    att_pair(2, 1)
    att_pair(2, 2)
    ag_y[2].start()
    proj(1)
    proj(2)

    f_a = remote(f0.at[0, pl.ds(0, C)], arr.at[pl.ds(0, C)], f_s.at[0], f_r.at[0], queue=q - 1)
    f_b = remote(
        f0.at[0, pl.ds(C, TOK - C)], arr.at[pl.ds(C, TOK - C)], f_s.at[1], f_r.at[1], queue=q - 1
    )
    fresh = pltpu.make_async_copy(fresh_hbm, arr, fresh_sem)

    @pl.when(q == nq - 1)
    def _():
        fresh.start()

    u = final(0)
    f0[0, pl.ds(0, C)] = u.astype(BF)
    f0f[pl.ds(0, C)] = u

    @pl.when(q > 0)
    def _():
        f_a.start()

    u = final(1)
    f0[0, pl.ds(C, TOK - C)] = u[: TOK - C].astype(BF)
    f0f[pl.ds(C, TOK - C)] = u[: TOK - C]
    out_ref[pl.ds(0, 2 * C - TOK)] = u[TOK - C :].astype(BF)

    @pl.when(q > 0)
    def _():
        f_b.start()

    share = TOK // nq

    def fin_copy(i):
        return remote(finsrc.at[i], findst, fin_s.at[i], fin_r.at[0], queue=i)

    @pl.when(q == 0)
    def _():
        f0f[pl.ds(TOK, 16)] = jnp.zeros((16, W), F32)
        for i in range(nq):
            finsrc[i] = f0f[pl.ds(i * share, 16)].astype(BF)

        def go(i, _):
            fin_copy(i).start()
            return 0

        pl.semaphore_wait(here, nq - 1)
        lax.fori_loop(1, nq, go, 0)

    out_ref[pl.ds(2 * C - TOK, C)] = final(2).astype(BF)

    @pl.when(q > 0)
    def _():
        f_a.wait_send()
        f_b.wait_send()
        fin_copy(0).wait_recv()
        fin_ref[...] = findst[pl.ds(0, share)]

    @pl.when(q == 0)
    def _():
        fin_ref[...] = finsrc[0, pl.ds(0, share)]

        def done(i, _):
            fin_copy(i).wait_send()
            return 0

        lax.fori_loop(1, nq, done, 0)

    @pl.when(q < nq - 1)
    def _():
        kv_k.wait_send()
        kv_v.wait_send()
        f_a.wait_recv()
        f_b.wait_recv()

    @pl.when(q == nq - 1)
    def _():
        fresh.wait()

    out_ref[pl.ds(TOK, TOK)] = arr[...]
    for c in (*wo_y, *wo_sib, *ag_y):
        c.wait_send()
    for r in range(NC):
        for _, c in rs[r]:
            c.wait_send()


def solution(mesh):
    nq = mesh.shape["queue"]

    def step(latents, fresh_noise, levels, frame_counts, modulation, w_qkv, w_out, sampler_coef):
        anyspace = pl.BlockSpec(memory_space=pl.ANY)
        smem = pl.BlockSpec(memory_space=pltpu.SMEM)
        vmem = pl.BlockSpec(memory_space=pltpu.VMEM)
        dma = pltpu.SemaphoreType.DMA
        return pl.pallas_call(
            lambda *refs: kernel(nq, *refs),
            out_shape=(pltpu.VMEM((ROWS, W), BF), pltpu.VMEM((TOK // nq, W), BF)),
            in_specs=[smem, smem, smem] + [anyspace] * 5,
            out_specs=(vmem, vmem),
            scratch_shapes=[
                pltpu.VMEM((ROWS, D), BF),
                pltpu.VMEM((3,) + modulation.shape[1:], F32),
                pltpu.VMEM((D, 3 * W), BF),
                pltpu.VMEM((ROWS, D), BF),
                pltpu.VMEM((ROWS, W), BF),
                pltpu.VMEM((ROWS, W), BF),
                pltpu.VMEM((W, ROWS), BF),
                pltpu.VMEM((TOK, W), BF),
                pltpu.VMEM((TOK, W), BF),
                pltpu.VMEM((W, TOK), BF),
                pltpu.VMEM((NX, 2 * W, W), BF),
                pltpu.VMEM((2, W, W), BF),
                pltpu.VMEM((NC, C, 2 * W), BF),
                pltpu.VMEM((NC, C, W), F32),
                pltpu.VMEM((NC, 3, C, W), BF),
                pltpu.VMEM((NC, 3, C, W), BF),
                pltpu.VMEM((2, TOK, W), BF),
                pltpu.VMEM((TOK + 16, W), F32),
                pltpu.VMEM((TOK, W), BF),
                pltpu.VMEM((nq, 16, W), BF),
                pltpu.VMEM((16, W), BF),
                dma((12,)), dma((2,)), dma((2,)), dma((4,)), dma((4,)),
                dma((NC,)), dma((NC,)), dma((NC, 3)), dma((NC, 3)),
                dma((2,)), dma((2,)), dma((nq,)), dma((1,)), dma, pltpu.SemaphoreType.REGULAR,
            ],
            compiler_params=pltpu.CompilerParams(
                collective_id=0, has_side_effects=True, vmem_limit_bytes=56 * 1024 * 1024
            ),
        )(
            levels, frame_counts, sampler_coef, latents, modulation,
            jnp.transpose(w_qkv, (1, 0, 2)), w_out, fresh_noise,
        )

    return jax.shard_map(
        step,
        mesh=mesh,
        in_specs=(
            P("queue", None), P(None, "tp"), P("queue"), P("queue"), P(),
            P(None, None, "tp"), P("tp", None), P(),
        ),
        out_specs=(P("queue", "tp"), P("queue", "tp")),
        check_vma=False,
    )
```

```python
import jax
import jax.numpy as jnp
from jax import lax
from jax.experimental import pallas as pl
from jax.experimental.pallas import tpu as pltpu
from jax.sharding import PartitionSpec as P

MESH = pl.DeviceIdType.MESH
BF = jnp.bfloat16
F32 = jnp.float32
D = 3072
W = 384
ROWS = 384
TOK = 192
NX = 4
C = 128
NC = 3
BIG = 1e30


def kernel(
    nq, levels, counts, coef, lat_hbm, mod_hbm, wqkv_hbm, wout_hbm, fresh_hbm,
    out_ref, fin_ref,
    lat, mod, wbuf, normed, qbuf, kown, vt, kpri, vpri, vtp, wo, wst, ag,
    acc, osend, orecv, rsend, rrecv, f0, f0f, arr, finsrc, findst,
    ld_sem, kv_s, kv_r, wo_s, wo_r, ag_s, ag_r, o_s, o_r, rs_s, rs_r, f_s, f_r, fin_s, fin_r, fresh_sem, here,
):
    q = lax.axis_index("queue")
    t = lax.axis_index("tp")
    x = lax.rem(t, NX)
    y = t // NX
    xr, xl, xo = lax.rem(x + 1, NX), lax.rem(x + 3, NX), lax.rem(x + 2, NX)
    right, left, opposite = y * NX + xr, y * NX + xl, y * NX + xo
    ypeer = (1 - y) * NX + x
    core = lax.rem(q, 2)
    sib = q + 1 - 2 * core
    q_other = q + 2 - 4 * (lax.rem(q, 4) // 2)

    def load(src, dst, i):
        return pltpu.make_async_copy(src, dst, ld_sem.at[i])

    def remote(src, dst, ss, rs, **dev):
        return pltpu.make_async_remote_copy(
            src_ref=src, dst_ref=dst, send_sem=ss, recv_sem=rs, device_id=dev, device_id_type=MESH
        )

    ld_f1 = load(lat_hbm.at[pl.ds(TOK, TOK)], lat.at[pl.ds(TOK, TOK)], 0)
    n_levels = mod_hbm.shape[0]
    first = jnp.clip(q * (n_levels - 1) // (nq - 1) - 1, 0, n_levels - 3)
    ld_mod = load(mod_hbm.at[pl.ds(first, 3)], mod, 1)
    ld_k = load(wqkv_hbm.at[1], wbuf.at[:, pl.ds(0, W)], 2)
    ld_v = load(wqkv_hbm.at[2], wbuf.at[:, pl.ds(W, W)], 3)
    ld_f0 = load(lat_hbm.at[pl.ds(0, TOK)], lat.at[pl.ds(0, TOK)], 4)
    ld_q = load(wqkv_hbm.at[0], wbuf.at[:, pl.ds(2 * W, W)], 5)

    def col(block):
        return pl.ds(pl.multiple_of(block * W, 128), W)

    def wblock(half, k):
        return wout_hbm.at[:, col(half * NX + k)]

    ld_o = [load(wblock(y, k), wo.at[k, pl.ds(0, W)], 6 + k) for k in range(NX)]
    ld_w = [load(wblock(1 - y, 2 * core + i), wst.at[i], 10 + i) for i in range(2)]
    for c in (ld_f1, ld_mod, *ld_w, ld_k, ld_v, ld_f0, ld_q, *ld_o):
        c.start()

    barrier = pltpu.get_barrier_semaphore()

    def hello(**dev):
        pl.semaphore_signal(barrier, inc=1, device_id=dev, device_id_type=MESH)

    for peer in (right, left, opposite, ypeer):
        hello(tp=peer)
    hello(tp=ypeer, queue=q_other)

    @pl.when(q == 0)
    def _():
        def greet(i, _):
            hello(queue=i)
            return 0

        lax.fori_loop(1, nq, greet, 0)

    @pl.when(q > 0)
    def _():
        hello(queue=q - 1)

        @pl.when(q < nq - 1)
        def _():
            hello(queue=q + 1)

    def meet():
        @pl.when(q == 0)
        def _():
            pl.semaphore_wait(barrier, 6)

        @pl.when(q == 1)
        def _():
            pl.semaphore_wait(barrier, 7)

        @pl.when((q > 1) & (q < nq - 1))
        def _():
            pl.semaphore_wait(barrier, 8)

        @pl.when(q == nq - 1)
        def _():
            pl.semaphore_wait(barrier, 7)

        @pl.when(q > 0)
        def _():
            pl.semaphore_signal(here, inc=1, device_id={"queue": 0}, device_id_type=MESH)

    wo_y, wo_sib = [], []
    for i in range(2):
        k = 2 * core + i
        low = wo.at[k, pl.ds(W, W)]
        wo_y.append(remote(wst.at[i], low, wo_s.at[i], wo_r.at[i], tp=ypeer, queue=(q, q_other)[i]))
        wo_sib.append(remote(low, low, wo_s.at[2 + i], wo_r.at[2 + i], queue=sib))

    level = levels[0]
    count = counts[0]
    full = count == 2
    c_lat = coef[0, level]
    c_out = coef[1, level]

    def norm(start):
        table = mod[jnp.clip(level - first, 0, 2)]
        gain = 1.0 + table[1:2]
        shift = table[0:1]

        def step(i, _):
            rows = pl.ds(pl.multiple_of(start + i * 16, 16), 16)
            v = lat[rows, :].astype(F32)
            d = v - jnp.mean(v, axis=1, keepdims=True)
            s = jnp.mean(d * d, axis=1, keepdims=True)
            normed[rows, :] = (d * lax.rsqrt(s + 1e-6) * gain + shift).astype(BF)
            return 0

        lax.fori_loop(0, TOK // 16, step, 0, unroll=2)

    def mm(start, rows, lo, width):
        return jnp.dot(
            normed[pl.ds(start, rows), :], wbuf[:, pl.ds(lo, width)], preferred_element_type=F32
        ).astype(BF)

    kv_k = remote(kown.at[pl.ds(TOK, TOK)], kpri, kv_s.at[0], kv_r.at[0], queue=q + 1)
    kv_v = remote(f0.at[1], vpri, kv_s.at[1], kv_r.at[1], queue=q + 1)

    ld_f1.wait()
    ld_mod.wait()
    meet()
    for c, l in zip(wo_y, ld_w):
        l.wait()
        c.start()
    norm(TOK)
    ld_k.wait()
    ld_v.wait()
    kown[pl.ds(TOK, TOK), pl.ds(0, 256)] = mm(TOK, TOK, 0, 256)
    mid = mm(TOK, TOK, 256, 256)
    kown[pl.ds(TOK, TOK), pl.ds(256, 128)] = mid[:, :128]

    @pl.when(q < nq - 1)
    def _():
        kv_k.start()

    f0[1, :, pl.ds(0, 128)] = mid[:, 128:]
    f0[1, :, pl.ds(128, 256)] = mm(TOK, TOK, 512, 256)

    @pl.when(q < nq - 1)
    def _():
        kv_v.start()

    @pl.when(q == 0)
    def _():
        kpri[...] = jnp.zeros_like(kpri)
        vpri[...] = jnp.zeros_like(vpri)

    ld_f0.wait()
    norm(0)

    ld_q.wait()
    qbuf[:, pl.ds(0, 256)] = mm(0, ROWS, 2 * W, 256) * BF(0.125)
    qbuf[:, pl.ds(256, 128)] = mm(0, ROWS, 2 * W + 256, 128) * BF(0.125)
    kown[pl.ds(0, TOK), pl.ds(0, 256)] = mm(0, TOK, 0, 256)
    mid = mm(0, TOK, 256, 256)
    kown[pl.ds(0, TOK), pl.ds(256, 128)] = mid[:, :128]
    v0 = jnp.concatenate([mid[:, 128:], mm(0, TOK, 512, 256)], axis=1)
    vt[...] = jnp.concatenate([v0, f0[1]], axis=0).T

    lane = lax.broadcasted_iota(jnp.int32, (C, C), 1)
    row = lax.broadcasted_iota(jnp.int32, (C, C), 0)
    has_prior = q > 0
    even = (lane < 64).astype(F32)
    odd = 1.0 - even

    def weigh(r, p):
        lanes = pl.ds(p * 128, 128)
        qp = qbuf[pl.ds(r * C, C), lanes].astype(F32)
        qs = jnp.concatenate([qp * even, qp * odd], axis=0).astype(BF)
        nt = (((1,), (1,)), ((), ()))
        so = lax.dot_general(kown[:, lanes], qs, nt, preferred_element_type=F32)
        sp = lax.dot_general(kpri[:, lanes], qs, nt, preferred_element_type=F32)
        s0, s1 = so[:TOK], so[TOK:]
        m0 = jnp.where(full, jnp.max(s0, axis=0, keepdims=True), -BIG)
        m1 = jnp.max(s1, axis=0, keepdims=True)
        mp = jnp.where(has_prior, jnp.max(sp, axis=0, keepdims=True), -BIG)
        top = jnp.maximum(jnp.maximum(m0, m1), mp)
        e0 = jnp.exp(s0 - jnp.where(full, top, BIG))
        e1 = jnp.exp(s1 - top)
        ep = jnp.exp(sp - jnp.where(has_prior, top, BIG))
        total = (
            jnp.sum(e0, axis=0, keepdims=True)
            + jnp.sum(e1, axis=0, keepdims=True)
            + jnp.sum(ep, axis=0, keepdims=True)
        )
        inv = 1.0 / total
        w_own = jnp.concatenate([(e0 * inv).astype(BF), (e1 * inv).astype(BF)], axis=0)
        return w_own, (ep * inv).astype(BF)

    def attend(r, p, w_own, w_pri):
        lanes = pl.ds(p * 128, 128)
        o = jnp.dot(vt[lanes, :], w_own, preferred_element_type=F32)
        o = o + jnp.dot(vtp[lanes, :], w_pri, preferred_element_type=F32)
        ot = jnp.where(row < 64, o[:, :C], o[:, C:])
        ag[r, :, lanes] = ot.T.astype(BF)

    def att_pair(r, p):
        attend(r, p, *weigh(r, p))

    ag_y = [
        remote(ag.at[r, :, pl.ds(0, W)], ag.at[r, :, pl.ds(W, W)], ag_s.at[r], ag_r.at[r], tp=ypeer)
        for r in range(NC)
    ]
    half = C // 2
    top_half, low_half = pl.ds(0, half), pl.ds(half, half)
    opp = [
        (
            remote(osend.at[r, top_half], orecv.at[r, top_half], o_s.at[r, 0], o_r.at[r, 0], tp=right),
            remote(osend.at[r, low_half], orecv.at[r, low_half], o_s.at[r, 1], o_r.at[r, 1], tp=left),
        )
        for r in range(NC)
    ]
    rs = [
        [
            remote(rsend.at[r, i], rrecv.at[r, i], rs_s.at[r, i], rs_r.at[r, i], tp=dev)
            for i, dev in enumerate((right, left))
        ]
        for r in range(NC)
    ]

    def proj_opp(r):
        ag_y[r].wait_recv()
        osend[r] = jnp.dot(ag[r], wo[xo], preferred_element_type=F32).astype(BF)
        for c in opp[r]:
            c.start()

    def proj(r):
        a = ag[r]
        to_right = jnp.dot(a, wo[xr], preferred_element_type=F32)
        to_left = jnp.dot(a, wo[xl], preferred_element_type=F32)
        opp[r][0].wait_recv()
        rsend[r, 0, top_half] = (to_right[:half] + orecv[r, top_half].astype(F32)).astype(BF)
        rsend[r, 0, low_half] = to_right[half:].astype(BF)
        rs[r][0].start()
        opp[r][1].wait_recv()
        rsend[r, 1, top_half] = to_left[:half].astype(BF)
        rsend[r, 1, low_half] = (to_left[half:] + orecv[r, low_half].astype(F32)).astype(BF)
        rs[r][1].start()
        acc[r] = jnp.dot(a, wo[x], preferred_element_type=F32)

    def final(r):
        branch = acc[r]
        for i, c in enumerate(rs[r]):
            c.wait_recv()
            branch = branch + rrecv[r, i].astype(F32)
        cur = lat[pl.ds(r * C, C), col(t)].astype(F32)
        upd = c_lat * cur + c_out * (cur + branch)
        if r == 0:
            valid = full
        elif r == 2:
            valid = True
        else:
            valid = full | (lax.broadcasted_iota(jnp.int32, (C, W), 0) >= TOK - C)
        if valid is not True:
            upd = jnp.where(valid, upd, cur)
        return upd

    @pl.when(q > 0)
    def _():
        kv_k.wait_recv()

    got = weigh(0, 0)

    @pl.when(q > 0)
    def _():
        kv_v.wait_recv()

    vtp[...] = vpri[...].T
    nxt = weigh(0, 1)
    attend(0, 0, *got)
    last = weigh(0, 2)
    attend(0, 1, *nxt)
    attend(0, 2, *last)
    ag_y[0].start()
    for got, on in zip(wo_y, wo_sib):
        got.wait_recv()
        on.start()
    got = weigh(1, 0)
    nxt = weigh(1, 1)
    attend(1, 0, *got)
    last = weigh(1, 2)
    attend(1, 1, *nxt)
    attend(1, 2, *last)
    ag_y[1].start()
    for c in ld_o:
        c.wait()
    att_pair(2, 0)
    for c in wo_sib:
        c.wait_recv()
    proj_opp(0)
    nxt = weigh(2, 1)
    last = weigh(2, 2)
    attend(2, 1, *nxt)
    attend(2, 2, *last)
    ag_y[2].start()
    proj_opp(1)
    proj(0)
    proj_opp(2)
    proj(1)
    proj(2)

    f_a = remote(f0.at[0, pl.ds(0, C)], arr.at[pl.ds(0, C)], f_s.at[0], f_r.at[0], queue=q - 1)
    f_b = remote(
        f0.at[0, pl.ds(C, TOK - C)], arr.at[pl.ds(C, TOK - C)], f_s.at[1], f_r.at[1], queue=q - 1
    )
    fresh = pltpu.make_async_copy(fresh_hbm, arr, fresh_sem)

    @pl.when(q == nq - 1)
    def _():
        fresh.start()

    u = final(0)
    f0[0, pl.ds(0, C)] = u.astype(BF)
    f0f[pl.ds(0, C)] = u

    @pl.when(q > 0)
    def _():
        f_a.start()

    u = final(1)
    f0[0, pl.ds(C, TOK - C)] = u[: TOK - C].astype(BF)
    f0f[pl.ds(C, TOK - C)] = u[: TOK - C]
    out_ref[pl.ds(0, 2 * C - TOK)] = u[TOK - C :].astype(BF)

    @pl.when(q > 0)
    def _():
        f_b.start()

    share = TOK // nq

    def fin_copy(i):
        return remote(finsrc.at[i], findst, fin_s.at[i], fin_r.at[0], queue=i)

    @pl.when(q == 0)
    def _():
        f0f[pl.ds(TOK, 16)] = jnp.zeros((16, W), F32)
        for i in range(nq):
            finsrc[i] = f0f[pl.ds(i * share, 16)].astype(BF)

        def go(i, _):
            fin_copy(i).start()
            return 0

        pl.semaphore_wait(here, nq - 1)
        lax.fori_loop(1, nq, go, 0)

    out_ref[pl.ds(2 * C - TOK, C)] = final(2).astype(BF)

    @pl.when(q > 0)
    def _():
        f_a.wait_send()
        f_b.wait_send()
        fin_copy(0).wait_recv()
        fin_ref[...] = findst[pl.ds(0, share)]

    @pl.when(q == 0)
    def _():
        fin_ref[...] = finsrc[0, pl.ds(0, share)]

        def done(i, _):
            fin_copy(i).wait_send()
            return 0

        lax.fori_loop(1, nq, done, 0)

    @pl.when(q < nq - 1)
    def _():
        kv_k.wait_send()
        kv_v.wait_send()
        f_a.wait_recv()
        f_b.wait_recv()

    @pl.when(q == nq - 1)
    def _():
        fresh.wait()

    out_ref[pl.ds(TOK, TOK)] = arr[...]
    for c in (*wo_y, *wo_sib, *ag_y):
        c.wait_send()
    for r in range(NC):
        for c in (*opp[r], *rs[r]):
            c.wait_send()


def solution(mesh):
    nq = mesh.shape["queue"]

    def step(latents, fresh_noise, levels, frame_counts, modulation, w_qkv, w_out, sampler_coef):
        anyspace = pl.BlockSpec(memory_space=pl.ANY)
        smem = pl.BlockSpec(memory_space=pltpu.SMEM)
        vmem = pl.BlockSpec(memory_space=pltpu.VMEM)
        dma = pltpu.SemaphoreType.DMA
        return pl.pallas_call(
            lambda *refs: kernel(nq, *refs),
            out_shape=(pltpu.VMEM((ROWS, W), BF), pltpu.VMEM((TOK // nq, W), BF)),
            in_specs=[smem, smem, smem] + [anyspace] * 5,
            out_specs=(vmem, vmem),
            scratch_shapes=[
                pltpu.VMEM((ROWS, D), BF),
                pltpu.VMEM((3,) + modulation.shape[1:], F32),
                pltpu.VMEM((D, 3 * W), BF),
                pltpu.VMEM((ROWS, D), BF),
                pltpu.VMEM((ROWS, W), BF),
                pltpu.VMEM((ROWS, W), BF),
                pltpu.VMEM((W, ROWS), BF),
                pltpu.VMEM((TOK, W), BF),
                pltpu.VMEM((TOK, W), BF),
                pltpu.VMEM((W, TOK), BF),
                pltpu.VMEM((NX, 2 * W, W), BF),
                pltpu.VMEM((2, W, W), BF),
                pltpu.VMEM((NC, C, 2 * W), BF),
                pltpu.VMEM((NC, C, W), F32),
                pltpu.VMEM((NC, C, W), BF),
                pltpu.VMEM((NC, C, W), BF),
                pltpu.VMEM((NC, 2, C, W), BF),
                pltpu.VMEM((NC, 2, C, W), BF),
                pltpu.VMEM((2, TOK, W), BF),
                pltpu.VMEM((TOK + 16, W), F32),
                pltpu.VMEM((TOK, W), BF),
                pltpu.VMEM((nq, 16, W), BF),
                pltpu.VMEM((16, W), BF),
                dma((12,)), dma((2,)), dma((2,)), dma((4,)), dma((4,)),
                dma((NC,)), dma((NC,)), dma((NC, 2)), dma((NC, 2)), dma((NC, 2)), dma((NC, 2)),
                dma((2,)), dma((2,)), dma((nq,)), dma((1,)), dma, pltpu.SemaphoreType.REGULAR,
            ],
            compiler_params=pltpu.CompilerParams(
                collective_id=0, has_side_effects=True, vmem_limit_bytes=56 * 1024 * 1024
            ),
        )(
            levels, frame_counts, sampler_coef, latents, modulation,
            jnp.transpose(w_qkv, (1, 0, 2)), w_out, fresh_noise,
        )

    return jax.shard_map(
        step,
        mesh=mesh,
        in_specs=(
            P("queue", None), P(None, "tp"), P("queue"), P("queue"), P(),
            P(None, None, "tp"), P("tp", None), P(),
        ),
        out_specs=(P("queue", "tp"), P("queue", "tp")),
        check_vma=False,
    )
```

```python
import jax
import jax.numpy as jnp
from jax import lax
from jax.experimental import pallas as pl
from jax.experimental.pallas import tpu as pltpu
from jax.sharding import PartitionSpec as P

MESH = pl.DeviceIdType.MESH
BF = jnp.bfloat16
F32 = jnp.float32
D = 3072
W = 384
ROWS = 384
TOK = 192
NX = 4
C = 128
NC = 3
BIG = 1e30


def kernel(
    nq, levels, counts, coef, lat_hbm, mod_hbm, wqkv_hbm, wout_hbm, fresh_hbm,
    out_ref, fin_ref,
    lat, mod, wbuf, normed, qbuf, kown, vt, kpri, vpri, vtp, wo, wst, ag,
    acc, osend, orecv, rsend, rrecv, f0, f0f, arr, finsrc, findst,
    ld_sem, kv_s, kv_r, wo_s, wo_r, ag_s, ag_r, o_s, o_r, rs_s, rs_r, f_s, f_r, fin_s, fin_r, fresh_sem, here,
):
    q = lax.axis_index("queue")
    t = lax.axis_index("tp")
    x = lax.rem(t, NX)
    y = t // NX
    xr, xl, xo = lax.rem(x + 1, NX), lax.rem(x + 3, NX), lax.rem(x + 2, NX)
    right, left, opposite = y * NX + xr, y * NX + xl, y * NX + xo
    ypeer = (1 - y) * NX + x
    core = lax.rem(q, 2)
    sib = q + 1 - 2 * core
    q_other = q + 2 - 4 * (lax.rem(q, 4) // 2)

    def load(src, dst, i):
        return pltpu.make_async_copy(src, dst, ld_sem.at[i])

    def remote(src, dst, ss, rs, **dev):
        return pltpu.make_async_remote_copy(
            src_ref=src, dst_ref=dst, send_sem=ss, recv_sem=rs, device_id=dev, device_id_type=MESH
        )

    ld_f1 = load(lat_hbm.at[pl.ds(TOK, TOK)], lat.at[pl.ds(TOK, TOK)], 0)
    n_levels = mod_hbm.shape[0]
    first = jnp.clip(q * (n_levels - 1) // (nq - 1) - 1, 0, n_levels - 3)
    ld_mod = load(mod_hbm.at[pl.ds(first, 3)], mod, 1)
    ld_k = load(wqkv_hbm.at[1], wbuf.at[:, pl.ds(0, W)], 2)
    ld_v = load(wqkv_hbm.at[2], wbuf.at[:, pl.ds(W, W)], 3)
    ld_f0 = load(lat_hbm.at[pl.ds(0, TOK)], lat.at[pl.ds(0, TOK)], 4)
    ld_q = load(wqkv_hbm.at[0], wbuf.at[:, pl.ds(2 * W, W)], 5)

    def col(block):
        return pl.ds(pl.multiple_of(block * W, 128), W)

    def wblock(half, k):
        return wout_hbm.at[:, col(half * NX + k)]

    ld_o = [load(wblock(y, k), wo.at[k, pl.ds(0, W)], 6 + k) for k in range(NX)]
    ld_w = [load(wblock(1 - y, 2 * core + i), wst.at[i], 10 + i) for i in range(2)]
    for c in (ld_f1, ld_mod, *ld_w, ld_k, ld_v, ld_f0, ld_q, *ld_o):
        c.start()

    barrier = pltpu.get_barrier_semaphore()

    def hello(**dev):
        pl.semaphore_signal(barrier, inc=1, device_id=dev, device_id_type=MESH)

    for peer in (right, left, opposite, ypeer):
        hello(tp=peer)
    hello(tp=ypeer, queue=q_other)

    @pl.when(q == 0)
    def _():
        def greet(i, _):
            hello(queue=i)
            return 0

        lax.fori_loop(1, nq, greet, 0)

    @pl.when(q > 0)
    def _():
        hello(queue=q - 1)

        @pl.when(q < nq - 1)
        def _():
            hello(queue=q + 1)

    def meet():
        @pl.when(q == 0)
        def _():
            pl.semaphore_wait(barrier, 6)

        @pl.when(q == 1)
        def _():
            pl.semaphore_wait(barrier, 7)

        @pl.when((q > 1) & (q < nq - 1))
        def _():
            pl.semaphore_wait(barrier, 8)

        @pl.when(q == nq - 1)
        def _():
            pl.semaphore_wait(barrier, 7)

        @pl.when(q > 0)
        def _():
            pl.semaphore_signal(here, inc=1, device_id={"queue": 0}, device_id_type=MESH)

    wo_y, wo_sib = [], []
    for i in range(2):
        k = 2 * core + i
        low = wo.at[k, pl.ds(W, W)]
        wo_y.append(remote(wst.at[i], low, wo_s.at[i], wo_r.at[i], tp=ypeer, queue=(q, q_other)[i]))
        wo_sib.append(remote(low, low, wo_s.at[2 + i], wo_r.at[2 + i], queue=sib))

    level = levels[0]
    count = counts[0]
    full = count == 2
    c_lat = coef[0, level]
    c_out = coef[1, level]

    def norm(start):
        table = mod[jnp.clip(level - first, 0, 2)]
        gain = 1.0 + table[1:2]
        shift = table[0:1]

        def step(i, _):
            rows = pl.ds(pl.multiple_of(start + i * 16, 16), 16)
            v = lat[rows, :].astype(F32)
            d = v - jnp.mean(v, axis=1, keepdims=True)
            s = jnp.mean(d * d, axis=1, keepdims=True)
            normed[rows, :] = (d * lax.rsqrt(s + 1e-6) * gain + shift).astype(BF)
            return 0

        lax.fori_loop(0, TOK // 16, step, 0, unroll=2)

    def mm(start, rows, lo, width):
        return jnp.dot(
            normed[pl.ds(start, rows), :], wbuf[:, pl.ds(lo, width)], preferred_element_type=F32
        ).astype(BF)

    kv_k = remote(kown.at[pl.ds(TOK, TOK)], kpri, kv_s.at[0], kv_r.at[0], queue=q + 1)
    kv_v = remote(f0.at[1], vpri, kv_s.at[1], kv_r.at[1], queue=q + 1)

    ld_f1.wait()
    ld_mod.wait()
    meet()
    for c, l in zip(wo_y, ld_w):
        l.wait()
        c.start()
    norm(TOK)
    ld_k.wait()
    ld_v.wait()
    kown[pl.ds(TOK, TOK), pl.ds(0, 256)] = mm(TOK, TOK, 0, 256)
    mid = mm(TOK, TOK, 256, 256)
    kown[pl.ds(TOK, TOK), pl.ds(256, 128)] = mid[:, :128]

    @pl.when(q < nq - 1)
    def _():
        kv_k.start()

    f0[1, :, pl.ds(0, 128)] = mid[:, 128:]
    f0[1, :, pl.ds(128, 256)] = mm(TOK, TOK, 512, 256)

    @pl.when(q < nq - 1)
    def _():
        kv_v.start()

    @pl.when(q == 0)
    def _():
        kpri[...] = jnp.zeros_like(kpri)
        vpri[...] = jnp.zeros_like(vpri)

    ld_f0.wait()
    norm(0)

    ld_q.wait()
    qbuf[:, pl.ds(0, 256)] = mm(0, ROWS, 2 * W, 256) * BF(0.125)
    qbuf[:, pl.ds(256, 128)] = mm(0, ROWS, 2 * W + 256, 128) * BF(0.125)
    kown[pl.ds(0, TOK), pl.ds(0, 256)] = mm(0, TOK, 0, 256)
    mid = mm(0, TOK, 256, 256)
    kown[pl.ds(0, TOK), pl.ds(256, 128)] = mid[:, :128]
    v0 = jnp.concatenate([mid[:, 128:], mm(0, TOK, 512, 256)], axis=1)
    vt[...] = jnp.concatenate([v0, f0[1]], axis=0).T

    lane = lax.broadcasted_iota(jnp.int32, (C, C), 1)
    row = lax.broadcasted_iota(jnp.int32, (C, C), 0)
    has_prior = q > 0
    even = (lane < 64).astype(F32)
    odd = 1.0 - even

    def weigh(r, p):
        lanes = pl.ds(p * 128, 128)
        qp = qbuf[pl.ds(r * C, C), lanes].astype(F32)
        qs = jnp.concatenate([qp * even, qp * odd], axis=0).astype(BF)
        nt = (((1,), (1,)), ((), ()))
        so = lax.dot_general(kown[:, lanes], qs, nt, preferred_element_type=F32)
        sp = lax.dot_general(kpri[:, lanes], qs, nt, preferred_element_type=F32)
        s0, s1 = so[:TOK], so[TOK:]
        m0 = jnp.where(full, jnp.max(s0, axis=0, keepdims=True), -BIG)
        m1 = jnp.max(s1, axis=0, keepdims=True)
        mp = jnp.where(has_prior, jnp.max(sp, axis=0, keepdims=True), -BIG)
        top = jnp.maximum(jnp.maximum(m0, m1), mp)
        e0 = jnp.exp(s0 - jnp.where(full, top, BIG))
        e1 = jnp.exp(s1 - top)
        ep = jnp.exp(sp - jnp.where(has_prior, top, BIG))
        total = (
            jnp.sum(e0, axis=0, keepdims=True)
            + jnp.sum(e1, axis=0, keepdims=True)
            + jnp.sum(ep, axis=0, keepdims=True)
        )
        inv = 1.0 / total
        w_own = jnp.concatenate([(e0 * inv).astype(BF), (e1 * inv).astype(BF)], axis=0)
        return w_own, (ep * inv).astype(BF)

    def attend(r, p, w_own, w_pri):
        lanes = pl.ds(p * 128, 128)
        o = jnp.dot(vt[lanes, :], w_own, preferred_element_type=F32)
        o = o + jnp.dot(vtp[lanes, :], w_pri, preferred_element_type=F32)
        ot = jnp.where(row < 64, o[:, :C], o[:, C:])
        ag[r, :, lanes] = ot.T.astype(BF)

    def att_pair(r, p):
        attend(r, p, *weigh(r, p))

    ag_y = [
        remote(ag.at[r, :, pl.ds(0, W)], ag.at[r, :, pl.ds(W, W)], ag_s.at[r], ag_r.at[r], tp=ypeer)
        for r in range(NC)
    ]
    half = C // 2
    top_half, low_half = pl.ds(0, half), pl.ds(half, half)
    opp = [
        (
            remote(osend.at[r, top_half], orecv.at[r, top_half], o_s.at[r, 0], o_r.at[r, 0], tp=right),
            remote(osend.at[r, low_half], orecv.at[r, low_half], o_s.at[r, 1], o_r.at[r, 1], tp=left),
        )
        for r in range(NC)
    ]
    rs = [
        [
            remote(rsend.at[r, i], rrecv.at[r, i], rs_s.at[r, i], rs_r.at[r, i], tp=dev)
            for i, dev in enumerate((right, left))
        ]
        for r in range(NC)
    ]

    def proj_opp(r):
        ag_y[r].wait_recv()
        osend[r] = jnp.dot(ag[r], wo[xo], preferred_element_type=F32).astype(BF)
        for c in opp[r]:
            c.start()

    def proj(r):
        a = ag[r]
        to_right = jnp.dot(a, wo[xr], preferred_element_type=F32)
        to_left = jnp.dot(a, wo[xl], preferred_element_type=F32)
        opp[r][0].wait_recv()
        rsend[r, 0, top_half] = (to_right[:half] + orecv[r, top_half].astype(F32)).astype(BF)
        rsend[r, 0, low_half] = to_right[half:].astype(BF)
        rs[r][0].start()
        opp[r][1].wait_recv()
        rsend[r, 1, top_half] = to_left[:half].astype(BF)
        rsend[r, 1, low_half] = (to_left[half:] + orecv[r, low_half].astype(F32)).astype(BF)
        rs[r][1].start()
        acc[r] = jnp.dot(a, wo[x], preferred_element_type=F32)

    def final(r):
        branch = acc[r]
        for i, c in enumerate(rs[r]):
            c.wait_recv()
            branch = branch + rrecv[r, i].astype(F32)
        cur = lat[pl.ds(r * C, C), col(t)].astype(F32)
        upd = c_lat * cur + c_out * (cur + branch)
        if r == 0:
            valid = full
        elif r == 2:
            valid = True
        else:
            valid = full | (lax.broadcasted_iota(jnp.int32, (C, W), 0) >= TOK - C)
        if valid is not True:
            upd = jnp.where(valid, upd, cur)
        return upd

    @pl.when(q > 0)
    def _():
        kv_k.wait_recv()

    got = weigh(0, 0)

    @pl.when(q > 0)
    def _():
        kv_v.wait_recv()

    vtp[...] = vpri[...].T
    nxt = weigh(0, 1)
    attend(0, 0, *got)
    last = weigh(0, 2)
    attend(0, 1, *nxt)
    attend(0, 2, *last)
    ag_y[0].start()
    for got, on in zip(wo_y, wo_sib):
        got.wait_recv()
        on.start()
    got = weigh(1, 0)
    nxt = weigh(1, 1)
    attend(1, 0, *got)
    last = weigh(1, 2)
    attend(1, 1, *nxt)
    attend(1, 2, *last)
    ag_y[1].start()
    for c in ld_o:
        c.wait()
    att_pair(2, 0)
    for c in wo_sib:
        c.wait_recv()
    proj_opp(0)
    nxt = weigh(2, 1)
    last = weigh(2, 2)
    attend(2, 1, *nxt)
    attend(2, 2, *last)
    ag_y[2].start()
    proj_opp(1)
    proj(0)
    proj_opp(2)
    proj(1)

    f_a = remote(f0.at[0, pl.ds(0, C)], arr.at[pl.ds(0, C)], f_s.at[0], f_r.at[0], queue=q - 1)
    f_b = remote(
        f0.at[0, pl.ds(C, TOK - C)], arr.at[pl.ds(C, TOK - C)], f_s.at[1], f_r.at[1], queue=q - 1
    )
    fresh = pltpu.make_async_copy(fresh_hbm, arr, fresh_sem)

    @pl.when(q == nq - 1)
    def _():
        fresh.start()

    u = final(0)
    f0[0, pl.ds(0, C)] = u.astype(BF)
    f0f[pl.ds(0, C)] = u

    @pl.when(q > 0)
    def _():
        f_a.start()

    proj(2)
    u = final(1)
    f0[0, pl.ds(C, TOK - C)] = u[: TOK - C].astype(BF)
    f0f[pl.ds(C, TOK - C)] = u[: TOK - C]
    out_ref[pl.ds(0, 2 * C - TOK)] = u[TOK - C :].astype(BF)

    @pl.when(q > 0)
    def _():
        f_b.start()

    share = TOK // nq

    def fin_copy(i):
        return remote(finsrc.at[i], findst, fin_s.at[i], fin_r.at[0], queue=i)

    @pl.when(q == 0)
    def _():
        f0f[pl.ds(TOK, 16)] = jnp.zeros((16, W), F32)
        for i in range(nq):
            finsrc[i] = f0f[pl.ds(i * share, 16)].astype(BF)

        def go(i, _):
            fin_copy(i).start()
            return 0

        pl.semaphore_wait(here, nq - 1)
        lax.fori_loop(1, nq, go, 0)

    out_ref[pl.ds(2 * C - TOK, C)] = final(2).astype(BF)

    @pl.when(q > 0)
    def _():
        f_a.wait_send()
        f_b.wait_send()
        fin_copy(0).wait_recv()
        fin_ref[...] = findst[pl.ds(0, share)]

    @pl.when(q == 0)
    def _():
        fin_ref[...] = finsrc[0, pl.ds(0, share)]

        def done(i, _):
            fin_copy(i).wait_send()
            return 0

        lax.fori_loop(1, nq, done, 0)

    @pl.when(q < nq - 1)
    def _():
        kv_k.wait_send()
        kv_v.wait_send()
        f_a.wait_recv()
        f_b.wait_recv()

    @pl.when(q == nq - 1)
    def _():
        fresh.wait()

    out_ref[pl.ds(TOK, TOK)] = arr[...]
    for c in (*wo_y, *wo_sib, *ag_y):
        c.wait_send()
    for r in range(NC):
        for c in (*opp[r], *rs[r]):
            c.wait_send()


def solution(mesh):
    nq = mesh.shape["queue"]

    def step(latents, fresh_noise, levels, frame_counts, modulation, w_qkv, w_out, sampler_coef):
        anyspace = pl.BlockSpec(memory_space=pl.ANY)
        smem = pl.BlockSpec(memory_space=pltpu.SMEM)
        vmem = pl.BlockSpec(memory_space=pltpu.VMEM)
        dma = pltpu.SemaphoreType.DMA
        return pl.pallas_call(
            lambda *refs: kernel(nq, *refs),
            out_shape=(pltpu.VMEM((ROWS, W), BF), pltpu.VMEM((TOK // nq, W), BF)),
            in_specs=[smem, smem, smem] + [anyspace] * 5,
            out_specs=(vmem, vmem),
            scratch_shapes=[
                pltpu.VMEM((ROWS, D), BF),
                pltpu.VMEM((3,) + modulation.shape[1:], F32),
                pltpu.VMEM((D, 3 * W), BF),
                pltpu.VMEM((ROWS, D), BF),
                pltpu.VMEM((ROWS, W), BF),
                pltpu.VMEM((ROWS, W), BF),
                pltpu.VMEM((W, ROWS), BF),
                pltpu.VMEM((TOK, W), BF),
                pltpu.VMEM((TOK, W), BF),
                pltpu.VMEM((W, TOK), BF),
                pltpu.VMEM((NX, 2 * W, W), BF),
                pltpu.VMEM((2, W, W), BF),
                pltpu.VMEM((NC, C, 2 * W), BF),
                pltpu.VMEM((NC, C, W), F32),
                pltpu.VMEM((NC, C, W), BF),
                pltpu.VMEM((NC, C, W), BF),
                pltpu.VMEM((NC, 2, C, W), BF),
                pltpu.VMEM((NC, 2, C, W), BF),
                pltpu.VMEM((2, TOK, W), BF),
                pltpu.VMEM((TOK + 16, W), F32),
                pltpu.VMEM((TOK, W), BF),
                pltpu.VMEM((nq, 16, W), BF),
                pltpu.VMEM((16, W), BF),
                dma((12,)), dma((2,)), dma((2,)), dma((4,)), dma((4,)),
                dma((NC,)), dma((NC,)), dma((NC, 2)), dma((NC, 2)), dma((NC, 2)), dma((NC, 2)),
                dma((2,)), dma((2,)), dma((nq,)), dma((1,)), dma, pltpu.SemaphoreType.REGULAR,
            ],
            compiler_params=pltpu.CompilerParams(
                collective_id=0, has_side_effects=True, vmem_limit_bytes=56 * 1024 * 1024
            ),
        )(
            levels, frame_counts, sampler_coef, latents, modulation,
            jnp.transpose(w_qkv, (1, 0, 2)), w_out, fresh_noise,
        )

    return jax.shard_map(
        step,
        mesh=mesh,
        in_specs=(
            P("queue", None), P(None, "tp"), P("queue"), P("queue"), P(),
            P(None, None, "tp"), P("tp", None), P(),
        ),
        out_specs=(P("queue", "tp"), P("queue", "tp")),
        check_vma=False,
    )
```

```python
import jax
import jax.numpy as jnp
from jax import lax
from jax.experimental import pallas as pl
from jax.experimental.pallas import tpu as pltpu
from jax.sharding import PartitionSpec as P

MESH = pl.DeviceIdType.MESH
BF = jnp.bfloat16
F32 = jnp.float32
D = 3072
W = 384
ROWS = 384
TOK = 192
NX = 4
C = 128
NC = 3
BIG = 1e30


def kernel(
    nq, levels, counts, coef, lat_hbm, mod_hbm, wqkv_hbm, wout_hbm, fresh_hbm,
    out_ref, fin_ref,
    lat, mod, wbuf, normed, qbuf, kown, vt, kpri, vpri, vtp, wo, wst, ag,
    acc, osend, orecv, rsend, rrecv, f0, f0f, arr, finsrc, findst,
    ld_sem, kv_s, kv_r, wo_s, wo_r, ag_s, ag_r, o_s, o_r, rs_s, rs_r, f_s, f_r, fin_s, fin_r, fresh_sem, here,
):
    q = lax.axis_index("queue")
    t = lax.axis_index("tp")
    x = lax.rem(t, NX)
    y = t // NX
    xr, xl, xo = lax.rem(x + 1, NX), lax.rem(x + 3, NX), lax.rem(x + 2, NX)
    right, left, opposite = y * NX + xr, y * NX + xl, y * NX + xo
    ypeer = (1 - y) * NX + x
    core = lax.rem(q, 2)
    sib = q + 1 - 2 * core
    q_other = q + 2 - 4 * (lax.rem(q, 4) // 2)

    def load(src, dst, i):
        return pltpu.make_async_copy(src, dst, ld_sem.at[i])

    def remote(src, dst, ss, rs, **dev):
        return pltpu.make_async_remote_copy(
            src_ref=src, dst_ref=dst, send_sem=ss, recv_sem=rs, device_id=dev, device_id_type=MESH
        )

    ld_f1 = load(lat_hbm.at[pl.ds(TOK, TOK)], lat.at[pl.ds(TOK, TOK)], 0)
    n_levels = mod_hbm.shape[0]
    first = jnp.clip(q * (n_levels - 1) // (nq - 1) - 1, 0, n_levels - 3)
    ld_mod = load(mod_hbm.at[pl.ds(first, 3)], mod, 1)
    ld_k = load(wqkv_hbm.at[1], wbuf.at[:, pl.ds(0, W)], 2)
    ld_v = load(wqkv_hbm.at[2], wbuf.at[:, pl.ds(W, W)], 3)
    ld_f0 = load(lat_hbm.at[pl.ds(0, TOK)], lat.at[pl.ds(0, TOK)], 4)
    ld_q = load(wqkv_hbm.at[0], wbuf.at[:, pl.ds(2 * W, W)], 5)

    def col(block):
        return pl.ds(pl.multiple_of(block * W, 128), W)

    def wblock(half, k):
        return wout_hbm.at[:, col(half * NX + k)]

    ld_o = [load(wblock(y, k), wo.at[k, pl.ds(0, W)], 6 + k) for k in range(NX)]
    ld_w = [load(wblock(1 - y, 2 * core + i), wst.at[i], 10 + i) for i in range(2)]
    for c in (ld_f1, ld_mod, *ld_w, ld_k, ld_v, ld_f0, ld_q, *ld_o):
        c.start()

    barrier = pltpu.get_barrier_semaphore()

    def hello(**dev):
        pl.semaphore_signal(barrier, inc=1, device_id=dev, device_id_type=MESH)

    for peer in (right, left, opposite, ypeer):
        hello(tp=peer)
    hello(tp=ypeer, queue=q_other)

    @pl.when(q == 0)
    def _():
        def greet(i, _):
            hello(queue=i)
            return 0

        lax.fori_loop(1, nq, greet, 0)

    @pl.when(q > 0)
    def _():
        hello(queue=q - 1)

        @pl.when(q < nq - 1)
        def _():
            hello(queue=q + 1)

    def meet():
        @pl.when(q == 0)
        def _():
            pl.semaphore_wait(barrier, 6)

        @pl.when(q == 1)
        def _():
            pl.semaphore_wait(barrier, 7)

        @pl.when((q > 1) & (q < nq - 1))
        def _():
            pl.semaphore_wait(barrier, 8)

        @pl.when(q == nq - 1)
        def _():
            pl.semaphore_wait(barrier, 7)

        @pl.when(q > 0)
        def _():
            pl.semaphore_signal(here, inc=1, device_id={"queue": 0}, device_id_type=MESH)

    wo_y, wo_sib = [], []
    for i in range(2):
        k = 2 * core + i
        low = wo.at[k, pl.ds(W, W)]
        wo_y.append(remote(wst.at[i], low, wo_s.at[i], wo_r.at[i], tp=ypeer, queue=(q, q_other)[i]))
        wo_sib.append(remote(low, low, wo_s.at[2 + i], wo_r.at[2 + i], queue=sib))

    level = levels[0]
    count = counts[0]
    full = count == 2
    c_lat = coef[0, level]
    c_out = coef[1, level]

    def norm(start):
        table = mod[jnp.clip(level - first, 0, 2)]
        gain = 1.0 + table[1:2]
        shift = table[0:1]

        def step(i, _):
            rows = pl.ds(pl.multiple_of(start + i * 16, 16), 16)
            v = lat[rows, :].astype(F32)
            d = v - jnp.mean(v, axis=1, keepdims=True)
            s = jnp.mean(d * d, axis=1, keepdims=True)
            normed[rows, :] = (d * lax.rsqrt(s + 1e-6) * gain + shift).astype(BF)
            return 0

        lax.fori_loop(0, TOK // 16, step, 0, unroll=2)

    def mm(start, rows, lo, width):
        return jnp.dot(
            normed[pl.ds(start, rows), :], wbuf[:, pl.ds(lo, width)], preferred_element_type=F32
        ).astype(BF)

    kv_k = remote(kown.at[pl.ds(TOK, TOK)], kpri, kv_s.at[0], kv_r.at[0], queue=q + 1)
    kv_v = remote(f0.at[1], vpri, kv_s.at[1], kv_r.at[1], queue=q + 1)

    ld_f1.wait()
    ld_mod.wait()
    meet()
    for c, l in zip(wo_y, ld_w):
        l.wait()
        c.start()
    norm(TOK)
    ld_k.wait()
    ld_v.wait()
    kown[pl.ds(TOK, TOK), pl.ds(0, 256)] = mm(TOK, TOK, 0, 256)
    mid = mm(TOK, TOK, 256, 256)
    kown[pl.ds(TOK, TOK), pl.ds(256, 128)] = mid[:, :128]

    @pl.when(q < nq - 1)
    def _():
        kv_k.start()

    f0[1, :, pl.ds(0, 128)] = mid[:, 128:]
    f0[1, :, pl.ds(128, 256)] = mm(TOK, TOK, 512, 256)

    @pl.when(q < nq - 1)
    def _():
        kv_v.start()

    @pl.when(q == 0)
    def _():
        kpri[...] = jnp.zeros_like(kpri)
        vpri[...] = jnp.zeros_like(vpri)

    ld_f0.wait()
    norm(0)

    ld_q.wait()
    qbuf[:, pl.ds(0, 256)] = mm(0, ROWS, 2 * W, 256) * BF(0.125)
    qbuf[:, pl.ds(256, 128)] = mm(0, ROWS, 2 * W + 256, 128) * BF(0.125)
    kown[pl.ds(0, TOK), pl.ds(0, 256)] = mm(0, TOK, 0, 256)
    mid = mm(0, TOK, 256, 256)
    kown[pl.ds(0, TOK), pl.ds(256, 128)] = mid[:, :128]
    v0 = jnp.concatenate([mid[:, 128:], mm(0, TOK, 512, 256)], axis=1)
    vt[...] = jnp.concatenate([v0, f0[1]], axis=0).T

    lane = lax.broadcasted_iota(jnp.int32, (C, C), 1)
    row = lax.broadcasted_iota(jnp.int32, (C, C), 0)
    has_prior = q > 0
    even = (lane < 64).astype(F32)
    odd = 1.0 - even

    def weigh(r, p):
        lanes = pl.ds(p * 128, 128)
        qp = qbuf[pl.ds(r * C, C), lanes].astype(F32)
        qs = jnp.concatenate([qp * even, qp * odd], axis=0).astype(BF)
        nt = (((1,), (1,)), ((), ()))
        so = lax.dot_general(kown[:, lanes], qs, nt, preferred_element_type=F32)
        sp = lax.dot_general(kpri[:, lanes], qs, nt, preferred_element_type=F32)
        s0, s1 = so[:TOK], so[TOK:]
        m0 = jnp.where(full, jnp.max(s0, axis=0, keepdims=True), -BIG)
        m1 = jnp.max(s1, axis=0, keepdims=True)
        mp = jnp.where(has_prior, jnp.max(sp, axis=0, keepdims=True), -BIG)
        top = jnp.maximum(jnp.maximum(m0, m1), mp)
        e0 = jnp.exp(s0 - jnp.where(full, top, BIG))
        e1 = jnp.exp(s1 - top)
        ep = jnp.exp(sp - jnp.where(has_prior, top, BIG))
        total = (
            jnp.sum(e0, axis=0, keepdims=True)
            + jnp.sum(e1, axis=0, keepdims=True)
            + jnp.sum(ep, axis=0, keepdims=True)
        )
        inv = 1.0 / total
        w_own = jnp.concatenate([(e0 * inv).astype(BF), (e1 * inv).astype(BF)], axis=0)
        return w_own, (ep * inv).astype(BF)

    def attend(r, p, w_own, w_pri):
        lanes = pl.ds(p * 128, 128)
        o = jnp.dot(vt[lanes, :], w_own, preferred_element_type=F32)
        o = o + jnp.dot(vtp[lanes, :], w_pri, preferred_element_type=F32)
        ot = jnp.where(row < 64, o[:, :C], o[:, C:])
        ag[r, :, lanes] = ot.T.astype(BF)

    def att_pair(r, p):
        attend(r, p, *weigh(r, p))

    ag_y = [
        remote(ag.at[r, :, pl.ds(0, W)], ag.at[r, :, pl.ds(W, W)], ag_s.at[r], ag_r.at[r], tp=ypeer)
        for r in range(NC)
    ]
    half = C // 2
    top_half, low_half = pl.ds(0, half), pl.ds(half, half)
    opp = [
        (
            remote(osend.at[r, top_half], orecv.at[r, top_half], o_s.at[r, 0], o_r.at[r, 0], tp=right),
            remote(osend.at[r, low_half], orecv.at[r, low_half], o_s.at[r, 1], o_r.at[r, 1], tp=left),
        )
        for r in range(NC)
    ]
    rs = [
        [
            remote(rsend.at[r, i], rrecv.at[r, i], rs_s.at[r, i], rs_r.at[r, i], tp=dev)
            for i, dev in enumerate((right, left))
        ]
        for r in range(NC)
    ]

    def proj_opp(r):
        ag_y[r].wait_recv()
        osend[r] = jnp.dot(ag[r], wo[xo], preferred_element_type=F32).astype(BF)
        for c in opp[r]:
            c.start()

    def proj(r):
        a = ag[r]
        to_right = jnp.dot(a, wo[xr], preferred_element_type=F32)
        to_left = jnp.dot(a, wo[xl], preferred_element_type=F32)
        opp[r][0].wait_recv()
        rsend[r, 0, top_half] = (to_right[:half] + orecv[r, top_half].astype(F32)).astype(BF)
        rsend[r, 0, low_half] = to_right[half:].astype(BF)
        rs[r][0].start()
        opp[r][1].wait_recv()
        rsend[r, 1, top_half] = to_left[:half].astype(BF)
        rsend[r, 1, low_half] = (to_left[half:] + orecv[r, low_half].astype(F32)).astype(BF)
        rs[r][1].start()
        acc[r] = jnp.dot(a, wo[x], preferred_element_type=F32)

    def final(r):
        branch = acc[r]
        for i, c in enumerate(rs[r]):
            c.wait_recv()
            branch = branch + rrecv[r, i].astype(F32)
        cur = lat[pl.ds(r * C, C), col(t)].astype(F32)
        upd = c_lat * cur + c_out * (cur + branch)
        if r == 0:
            valid = full
        elif r == 2:
            valid = True
        else:
            valid = full | (lax.broadcasted_iota(jnp.int32, (C, W), 0) >= TOK - C)
        if valid is not True:
            upd = jnp.where(valid, upd, cur)
        return upd

    @pl.when(q > 0)
    def _():
        kv_k.wait_recv()

    got = weigh(0, 0)

    @pl.when(q > 0)
    def _():
        kv_v.wait_recv()

    vtp[...] = vpri[...].T
    nxt = weigh(0, 1)
    attend(0, 0, *got)
    last = weigh(0, 2)
    attend(0, 1, *nxt)
    attend(0, 2, *last)
    ag_y[0].start()
    for got, on in zip(wo_y, wo_sib):
        got.wait_recv()
        on.start()
    got = weigh(1, 0)
    nxt = weigh(1, 1)
    attend(1, 0, *got)
    last = weigh(1, 2)
    attend(1, 1, *nxt)
    attend(1, 2, *last)
    ag_y[1].start()
    for c in ld_o:
        c.wait()
    att_pair(2, 0)
    for c in wo_sib:
        c.wait_recv()
    proj_opp(0)
    nxt = weigh(2, 1)
    last = weigh(2, 2)
    attend(2, 1, *nxt)
    attend(2, 2, *last)
    ag_y[2].start()
    proj_opp(1)
    proj(0)
    proj_opp(2)
    proj(1)

    f_a = remote(f0.at[0, pl.ds(0, C)], arr.at[pl.ds(0, C)], f_s.at[0], f_r.at[0], queue=q - 1)
    f_b = remote(
        f0.at[0, pl.ds(C, TOK - C)], arr.at[pl.ds(C, TOK - C)], f_s.at[1], f_r.at[1], queue=q - 1
    )
    fresh = pltpu.make_async_copy(fresh_hbm, arr, fresh_sem)

    @pl.when(q == nq - 1)
    def _():
        fresh.start()

    u = final(0)
    f0[0, pl.ds(0, C)] = u.astype(BF)

    @pl.when(q > 0)
    def _():
        f_a.start()

    f0f[pl.ds(0, C)] = u

    proj(2)
    u = final(1)
    f0[0, pl.ds(C, TOK - C)] = u[: TOK - C].astype(BF)

    @pl.when(q > 0)
    def _():
        f_b.start()

    f0f[pl.ds(C, TOK - C)] = u[: TOK - C]
    out_ref[pl.ds(0, 2 * C - TOK)] = u[TOK - C :].astype(BF)

    share = TOK // nq

    def fin_copy(i):
        return remote(finsrc.at[i], findst, fin_s.at[i], fin_r.at[0], queue=i)

    @pl.when(q == 0)
    def _():
        f0f[pl.ds(TOK, 16)] = jnp.zeros((16, W), F32)
        for i in range(nq):
            finsrc[i] = f0f[pl.ds(i * share, 16)].astype(BF)

        def go(i, _):
            fin_copy(i).start()
            return 0

        pl.semaphore_wait(here, nq - 1)
        lax.fori_loop(1, nq, go, 0)

    out_ref[pl.ds(2 * C - TOK, C)] = final(2).astype(BF)

    @pl.when(q > 0)
    def _():
        f_a.wait_send()
        f_b.wait_send()
        fin_copy(0).wait_recv()
        fin_ref[...] = findst[pl.ds(0, share)]

    @pl.when(q == 0)
    def _():
        fin_ref[...] = finsrc[0, pl.ds(0, share)]

        def done(i, _):
            fin_copy(i).wait_send()
            return 0

        lax.fori_loop(1, nq, done, 0)

    @pl.when(q < nq - 1)
    def _():
        kv_k.wait_send()
        kv_v.wait_send()
        f_a.wait_recv()
        f_b.wait_recv()

    @pl.when(q == nq - 1)
    def _():
        fresh.wait()

    out_ref[pl.ds(TOK, TOK)] = arr[...]
    for c in (*wo_y, *wo_sib, *ag_y):
        c.wait_send()
    for r in range(NC):
        for c in (*opp[r], *rs[r]):
            c.wait_send()


def solution(mesh):
    nq = mesh.shape["queue"]

    def step(latents, fresh_noise, levels, frame_counts, modulation, w_qkv, w_out, sampler_coef):
        anyspace = pl.BlockSpec(memory_space=pl.ANY)
        smem = pl.BlockSpec(memory_space=pltpu.SMEM)
        vmem = pl.BlockSpec(memory_space=pltpu.VMEM)
        dma = pltpu.SemaphoreType.DMA
        return pl.pallas_call(
            lambda *refs: kernel(nq, *refs),
            out_shape=(pltpu.VMEM((ROWS, W), BF), pltpu.VMEM((TOK // nq, W), BF)),
            in_specs=[smem, smem, smem] + [anyspace] * 5,
            out_specs=(vmem, vmem),
            scratch_shapes=[
                pltpu.VMEM((ROWS, D), BF),
                pltpu.VMEM((3,) + modulation.shape[1:], F32),
                pltpu.VMEM((D, 3 * W), BF),
                pltpu.VMEM((ROWS, D), BF),
                pltpu.VMEM((ROWS, W), BF),
                pltpu.VMEM((ROWS, W), BF),
                pltpu.VMEM((W, ROWS), BF),
                pltpu.VMEM((TOK, W), BF),
                pltpu.VMEM((TOK, W), BF),
                pltpu.VMEM((W, TOK), BF),
                pltpu.VMEM((NX, 2 * W, W), BF),
                pltpu.VMEM((2, W, W), BF),
                pltpu.VMEM((NC, C, 2 * W), BF),
                pltpu.VMEM((NC, C, W), F32),
                pltpu.VMEM((NC, C, W), BF),
                pltpu.VMEM((NC, C, W), BF),
                pltpu.VMEM((NC, 2, C, W), BF),
                pltpu.VMEM((NC, 2, C, W), BF),
                pltpu.VMEM((2, TOK, W), BF),
                pltpu.VMEM((TOK + 16, W), F32),
                pltpu.VMEM((TOK, W), BF),
                pltpu.VMEM((nq, 16, W), BF),
                pltpu.VMEM((16, W), BF),
                dma((12,)), dma((2,)), dma((2,)), dma((4,)), dma((4,)),
                dma((NC,)), dma((NC,)), dma((NC, 2)), dma((NC, 2)), dma((NC, 2)), dma((NC, 2)),
                dma((2,)), dma((2,)), dma((nq,)), dma((1,)), dma, pltpu.SemaphoreType.REGULAR,
            ],
            compiler_params=pltpu.CompilerParams(
                collective_id=0, has_side_effects=True, vmem_limit_bytes=56 * 1024 * 1024
            ),
        )(
            levels, frame_counts, sampler_coef, latents, modulation,
            jnp.transpose(w_qkv, (1, 0, 2)), w_out, fresh_noise,
        )

    return jax.shard_map(
        step,
        mesh=mesh,
        in_specs=(
            P("queue", None), P(None, "tp"), P("queue"), P("queue"), P(),
            P(None, None, "tp"), P("tp", None), P(),
        ),
        out_specs=(P("queue", "tp"), P("queue", "tp")),
        check_vma=False,
    )
```
